32 devices in a mesh: hst: 16 (over z, x, core), tensor: 2 (over y).
Axes of the slice: x: 2, y: 2, z: 4, core: 2. Of those that a mesh axis runs over, the one named last changes fastest.
Arguments:
- ctx_query: bfloat16 [8192, 8192], P('hst', 'tensor'), may hold values from -60 to 60
- ctx_key: bfloat16 [8192, 1024], P('hst', 'tensor'), may hold values from -12 to 12
- context_value: bfloat16 [8192, 1024], P('hst', 'tensor'), may hold values from -6 to 6
- lengths: int32 [16], replicated, may hold values from 1 to 512, 6144 in all
- owner: int32 [1], replicated, may hold values from 0 to 15
- ask_query: bfloat16 [16, 256, 8192], P('hst', None, 'tensor'), may hold values from -60 to 60
- ask_key: bfloat16 [16, 256, 1024], P('hst', None, 'tensor'), may hold values from -12 to 12
- candidate_value_rows: bfloat16 [16, 256, 1024], P('hst', None, 'tensor'), may hold values from -6 to 6
- out_weight: bfloat16 [8192, 8192], P('tensor', 'hst'), may hold values from -0.0625 to 0.0625
Outputs:
- ctx_out: bfloat16 [8192, 8192], P('hst', 'tensor')
- layer_out: bfloat16 [256, 8192], P('tensor', 'hst')
The draws below stay inside these ranges and needn't reach their ends.
Inputs may be any that keep to these rules, and one draw needn't show every extreme that they name: `lengths`: every block has at least one valid slot and some block is full.
All inputs are finite; a program needn't handle non-finite values.
Results may differ from the reference program's by a relative error of at most 0.009.
Values may be sent and summed in bfloat16 or wider, within the bound.
No kernel may reach another device: no remote copies, remote signals or barrier semaphores. Data moves between devices by JAX's collectives and lax.ppermute only.
A program may use at most 384 MiB of HBM per device.

```python
import math
import jax
import jax.numpy as jnp
import numpy as np
from jax import lax

D = 8192
HQ = 64
KEY_VALUE_HEADS = 8
HEAD_SIZE = 128
BLK = 512
QUERY_ROW_COUNT = 256
CONTEXT_TOKENS = 8192
N_HST = 16


def draw_ctx_query(key, part):
    key = jax.random.fold_in(key, 11)
    base_offset = jnp.clip(jax.random.normal(key, (CONTEXT_TOKENS, HQ, HEAD_SIZE), jnp.float32), -4.0, 4.0) * 3.0
    return base_offset.reshape(CONTEXT_TOKENS, HQ * HEAD_SIZE).astype(jnp.bfloat16)


def draw_ctx_key(key, part):
    key = jax.random.fold_in(key, 23)
    first_piece = jax.random.fold_in(key, 0)
    base_offset = jnp.clip(jax.random.normal(first_piece, (CONTEXT_TOKENS, KEY_VALUE_HEADS, HEAD_SIZE), jnp.float32), -4.0, 4.0)
    return base_offset.reshape(CONTEXT_TOKENS, KEY_VALUE_HEADS * HEAD_SIZE).astype(jnp.bfloat16)


def draw_ask_query(key, part):
    key = jax.random.fold_in(key, 37)
    base_offset = jnp.clip(jax.random.normal(key, (N_HST, QUERY_ROW_COUNT, HQ, HEAD_SIZE), jnp.float32), -4.0, 4.0) * 3.0
    return base_offset.reshape(N_HST, QUERY_ROW_COUNT, HQ * HEAD_SIZE).astype(jnp.bfloat16)


def draw_ask_key(key, part):
    key = jax.random.fold_in(key, 41)
    first_piece = jax.random.fold_in(key, 0)
    base_offset = jnp.clip(jax.random.normal(first_piece, (N_HST, QUERY_ROW_COUNT, KEY_VALUE_HEADS, HEAD_SIZE), jnp.float32), -4.0, 4.0) * 1.4
    return base_offset.reshape(N_HST, QUERY_ROW_COUNT, KEY_VALUE_HEADS * HEAD_SIZE).astype(jnp.bfloat16)


def shard_levels(stream_key, extent, shards, smallest, top_value):
    gain, own = 1.0, jax.random.fold_in(stream_key, 6)
    for axis_at, parts in shards:
        heights = jnp.exp(jax.random.uniform(jax.random.fold_in(own, axis_at), (parts,), jnp.float32, smallest / len(shards), top_value / len(shards)))
        gain = gain * jnp.repeat(heights, extent[axis_at] // parts).reshape([-1 if axis == axis_at else 1 for axis in range(len(extent))])
    return gain


def profile(count, total, limit, skew):
    weights = [(1 << 20) // math.isqrt(standing ** skew) + 1 for standing in range(2, count + 1)]
    surplus, given = total - limit - (count - 1), [1] * (count - 1)
    while surplus > 0:
        candidates = [i for i in range(count - 1) if given[i] < limit]
        mass, remaining = sum([weights[i] for i in candidates]), surplus
        for i in candidates:
            more = min(limit - given[i], max(1, remaining * weights[i] // mass), surplus)
            given[i] = given[i] + more
            surplus = surplus - more
    return np.array([limit] + given)


def ragged_sizes(stream_key, count, total, bound, slope):
    if count == 2:
        one = jax.random.randint(stream_key, (), max(1, total - bound), min(bound, total - 1) + 1)
        return jnp.stack([one, total - one])
    tallies = jnp.asarray(profile(count, total, bound, slope), jnp.int32)
    couples = (count - 1) // 2
    donor, receiver = tallies[1:1 + 2 * couples:2], tallies[2:2 + 2 * couples:2]
    slack = jnp.minimum(donor - 1, bound - receiver)
    passed = jax.random.randint(jax.random.fold_in(stream_key, 1), (couples,), 0, 1 << 20) % (slack + 1)
    tallies = tallies.at[1:1 + 2 * couples:2].set(donor - passed).at[2:2 + 2 * couples:2].set(receiver + passed)
    return tallies[jax.random.permutation(jax.random.fold_in(stream_key, 2), count)]


def bell_draw(stream_key, shape, deviation, bound, cuts=(), kind=jnp.bfloat16):
    array = jax.random.normal(stream_key, shape, jnp.float32) * deviation
    if len(cuts) > 0:
        array = shard_levels(stream_key, shape, cuts, -0.22, 0.18) * array
    return jnp.clip(array, min=-bound, max=bound).astype(kind)


def setup_inputs(seed: int = 0) -> dict:
    seeds = jax.random.split(jax.random.key(seed), 10)
    ctx_query = draw_ctx_query(jax.random.fold_in(seeds[9], 71), 0)
    ctx_key = draw_ctx_key(jax.random.fold_in(seeds[9], 71), 0)
    context_value = bell_draw(seeds[2], (CONTEXT_TOKENS, KEY_VALUE_HEADS * HEAD_SIZE), 1.0, 6.0, ((0, 16), (1, 2)))
    lengths = ragged_sizes(seeds[3], N_HST, N_HST * BLK * 3 // 4, BLK, 1).astype(jnp.int32)
    owner = jax.random.randint(seeds[4], (1,), 0, N_HST).astype(jnp.int32)
    ask_query = draw_ask_query(jax.random.fold_in(seeds[9], 71), 0)
    ask_key = draw_ask_key(jax.random.fold_in(seeds[9], 71), 0)
    candidate_value_rows = bell_draw(seeds[7], (N_HST, QUERY_ROW_COUNT, KEY_VALUE_HEADS * HEAD_SIZE), 1.0, 6.0, ((0, 16), (2, 2)))
    out_weight = bell_draw(seeds[8], (HQ * HEAD_SIZE, D), (HQ * HEAD_SIZE) ** -0.5, 0.0625, ((0, 2), (1, 16)))
    return {"ctx_query": ctx_query, "ctx_key": ctx_key, "context_value": context_value, "lengths": lengths, "owner": owner, "ask_query": ask_query, "ask_key": ask_key, "candidate_value_rows": candidate_value_rows, "out_weight": out_weight}


masked_score = -1e+30

def partial_attend(queries, keys, values, allowed):
    rows = queries.shape[0]
    groups = keys.shape[1] // HEAD_SIZE
    query_heads = queries.astype(jnp.float32).reshape(rows, groups, -1, HEAD_SIZE)
    key_heads = keys.astype(jnp.float32).reshape(keys.shape[0], groups, HEAD_SIZE)
    value_heads = values.astype(jnp.float32).reshape(values.shape[0], groups, HEAD_SIZE)
    scores = jnp.einsum('rkgd,skd->rkgs', query_heads, key_heads) / math.sqrt(HEAD_SIZE)
    scores = jnp.where(allowed[:, None, None, :], scores, masked_score)
    peaks = lax.optimization_barrier(jnp.max(scores, axis=-1))
    weights = lax.optimization_barrier(jnp.exp(scores - peaks[..., None]).astype(jnp.bfloat16))
    weights = weights.astype(jnp.float32)
    totals = lax.optimization_barrier(jnp.sum(weights, axis=-1))
    outputs = jnp.einsum('rkgs,skd->rkgd', weights, value_heads)
    return (peaks.reshape(rows, -1), totals.reshape(rows, -1), outputs.reshape(rows, -1))

def normalize(outputs, totals):
    rows, heads = totals.shape
    return (outputs.reshape(rows, heads, -1) / totals[..., None]).reshape(rows, -1)

def reference(ctx_query, ctx_key, context_value, lengths, owner, ask_query, ask_key, candidate_value_rows, out_weight):
    positions = jnp.arange(BLK, dtype=jnp.int32)
    anchor_key = ctx_key[:BLK]
    anchor_value = context_value[:BLK]

    def encode_block(block):
        start = (block * BLK).astype(jnp.int32)
        queries = lax.dynamic_slice_in_dim(ctx_query, start, BLK, 0)
        own_key = lax.dynamic_slice_in_dim(ctx_key, start, BLK, 0)
        own_value = lax.dynamic_slice_in_dim(context_value, start, BLK, 0)
        own_len = lengths[block]
        anchor_ok = jnp.broadcast_to((positions[None, :] < lengths[0]) & (block > 0), (BLK, BLK))
        own_ok = (positions[None, :] <= positions[:, None]) & (positions[None, :] < own_len)
        allowed = jnp.concatenate([anchor_ok, own_ok], axis=1)
        keys_all = jnp.concatenate([anchor_key, own_key], axis=0)
        values_all = jnp.concatenate([anchor_value, own_value], axis=0)
        peaks, totals, outputs = partial_attend(queries, keys_all, values_all, allowed)
        result = jnp.where(positions[:, None] < own_len, normalize(outputs, totals), 0.0)
        return result.astype(jnp.bfloat16)
    blocks = jnp.arange(N_HST, dtype=jnp.int32)
    ctx_out = lax.map(encode_block, blocks).reshape(CONTEXT_TOKENS, HQ * HEAD_SIZE)
    chosen = owner[0]
    asked = lax.dynamic_index_in_dim(ask_query, chosen, 0, keepdims=False)
    ask_keys = lax.dynamic_index_in_dim(ask_key, chosen, 0, keepdims=False)
    ask_values = lax.dynamic_index_in_dim(candidate_value_rows, chosen, 0, keepdims=False)

    def read_block(block):
        start = (block * BLK).astype(jnp.int32)
        keys = lax.dynamic_slice_in_dim(ctx_key, start, BLK, 0)
        values = lax.dynamic_slice_in_dim(context_value, start, BLK, 0)
        allowed = jnp.broadcast_to((positions < lengths[block])[None, :], (QUERY_ROW_COUNT, BLK))
        return partial_attend(asked, keys, values, allowed)
    peaks_all, totals_all, outputs_all = lax.map(read_block, blocks)
    query_pos = jnp.arange(QUERY_ROW_COUNT, dtype=jnp.int32)
    self_peak, self_total, self_out = partial_attend(asked, ask_keys, ask_values, query_pos[None, :] <= query_pos[:, None])
    top = jnp.maximum(lax.optimization_barrier(jnp.max(peaks_all, axis=0)), self_peak)
    scales = jnp.exp(peaks_all - top[None])
    self_scale = jnp.exp(self_peak - top)
    totals = lax.optimization_barrier(jnp.sum(scales * totals_all, axis=0)) + self_scale * self_total
    outputs = lax.optimization_barrier(jnp.sum(outputs_all.reshape(N_HST, QUERY_ROW_COUNT, HQ, HEAD_SIZE) * scales[..., None], axis=0))
    outputs = outputs + self_out.reshape(QUERY_ROW_COUNT, HQ, HEAD_SIZE) * self_scale[..., None]
    answer = normalize(outputs.reshape(QUERY_ROW_COUNT, HQ * HEAD_SIZE), totals).astype(jnp.bfloat16)
    layer_out = jnp.dot(answer, out_weight, preferred_element_type=jnp.float32).astype(jnp.bfloat16)
    return (ctx_out, layer_out)
```

```python
import functools
import math

import jax
import jax.numpy as jnp
from jax import lax
from jax.experimental import pallas as pl
from jax.experimental.pallas import tpu as pltpu
from jax.sharding import PartitionSpec as P

HEAD_SIZE = 128
F32 = jnp.float32
BF16 = jnp.bfloat16
LOG_SCALE = math.log2(math.e) / math.sqrt(HEAD_SIZE)
VMEM_LIMIT = 56 * 2**20


masked_score = -1e30


def broadcast(block, axis, owner):
    block = jnp.where(lax.axis_index(axis) == owner, block, jnp.zeros_like(block))
    return lax.psum(block, axis)


def combined_all(array, axis, combine):
    everything = jax.tree.map(lambda part: lax.all_gather(part, axis), array)
    first = jax.tree.map(lambda part: part[0], everything)

    def hop(k, so_far):
        return combine(so_far, jax.tree.map(lambda part: part[k], everything))

    return lax.fori_loop(1, lax.axis_size(axis), hop, first)


def partial_attend(queries, keys, values, allowed):
    rows = queries.shape[0]
    groups = keys.shape[1] // HEAD_SIZE
    query_heads = queries.reshape(rows, groups, -1, HEAD_SIZE)
    key_heads = keys.reshape(keys.shape[0], groups, HEAD_SIZE)
    value_heads = values.reshape(values.shape[0], groups, HEAD_SIZE)
    scores = jnp.einsum(
        "rkgd,skd->rkgs", query_heads, key_heads, preferred_element_type=jnp.float32
    ) / math.sqrt(HEAD_SIZE)
    scores = jnp.where(allowed[:, None, None, :], scores, masked_score)
    peaks = jnp.max(scores, axis=-1)
    weights = jnp.exp(scores - peaks[..., None]).astype(jnp.bfloat16)
    totals = jnp.sum(weights.astype(jnp.float32), axis=-1)
    outputs = jnp.einsum("rkgs,skd->rkgd", weights, value_heads, preferred_element_type=jnp.float32)
    return (peaks.reshape(rows, -1), totals.reshape(rows, -1), outputs.reshape(rows, -1))


def normalize(outputs, totals):
    rows, heads = totals.shape
    return (outputs.reshape(rows, heads, -1) / totals[..., None]).reshape(rows, -1)


def combine(first_piece, second_piece):
    rows, heads = first_piece[0].shape
    top = jnp.maximum(first_piece[0], second_piece[0])
    scale_one = jnp.exp(first_piece[0] - top)
    scale_two = jnp.exp(second_piece[0] - top)
    totals = scale_one * first_piece[1] + scale_two * second_piece[1]
    outputs = (
        first_piece[2].reshape(rows, heads, -1) * scale_one[..., None]
        + second_piece[2].reshape(rows, heads, -1) * scale_two[..., None]
    )
    return (top, totals, outputs.reshape(rows, -1))


def generic_body(
    ctx_query,
    ctx_key,
    context_value,
    lengths,
    owner,
    ask_query,
    ask_key,
    candidate_value_rows,
    out_weight,
):
    host = lax.axis_index("hst")
    anchor_key, anchor_value = (broadcast(ctx_key, "hst", 0), broadcast(context_value, "hst", 0))
    block_len = ctx_query.shape[0]
    own_len = lengths[host]
    anchor_len = lengths[0]
    keys_all = jnp.concatenate([anchor_key, ctx_key], axis=0)
    values_all = jnp.concatenate([anchor_value, context_value], axis=0)
    rows_each = min(512, block_len)
    columns = jnp.arange(block_len, dtype=jnp.int32)
    row_pos = 0 + jnp.arange(rows_each, dtype=jnp.int32)
    anchor_ok = jnp.broadcast_to(
        (columns[None, :] < anchor_len) & (host > 0), (rows_each, block_len)
    )
    own_ok = (columns[None, :] <= row_pos[:, None]) & (columns[None, :] < own_len)
    allowed = jnp.concatenate([anchor_ok, own_ok], axis=1)
    peaks, totals, outputs = partial_attend(ctx_query, keys_all, values_all, allowed)
    result = jnp.where(row_pos[:, None] < own_len, normalize(outputs, totals), 0.0)
    pieces = result.astype(jnp.bfloat16)
    chosen = owner[0]
    query_rows = ask_query.shape[1]
    query_pos = jnp.arange(query_rows, dtype=jnp.int32)
    causal = query_pos[None, :] <= query_pos[:, None]
    block_ok = jnp.broadcast_to((columns < own_len)[None, :], (query_rows, block_len))
    asked, ask_keys, ask_values = (
        broadcast(ask_query[0], "hst", chosen),
        broadcast(ask_key[0], "hst", chosen),
        broadcast(candidate_value_rows[0], "hst", chosen),
    )
    local = partial_attend(asked, ctx_key, context_value, block_ok)
    pending = partial_attend(asked, ask_keys, ask_values, causal)
    merged = combined_all(local, "hst", combine)
    merged = combine(merged, pending)
    answer = normalize(merged[2], merged[1]).astype(jnp.bfloat16)
    projected = jnp.dot(answer, out_weight, preferred_element_type=jnp.float32)
    layer_out = lax.psum_scatter(
        projected.astype(jnp.bfloat16), "tensor", scatter_dimension=0, tiled=True
    )
    return (pieces, layer_out)


def dot_t(a, b):
    return lax.dot_general(a, b, (((1,), (1,)), ((), ())), preferred_element_type=F32)


def swap(array, bit):
    return lax.ppermute(array, "hst", [(i, i ^ bit) for i in range(16)])


def call(kernel, out_shape, in_specs, out_specs, grid=(), scratch=(), prefetch=1, flops=0, data=0, aliases=None):
    return pl.pallas_call(
        kernel,
        grid_spec=pltpu.PrefetchScalarGridSpec(
            num_scalar_prefetch=prefetch, grid=grid, in_specs=in_specs, out_specs=out_specs, scratch_shapes=list(scratch)
        ),
        out_shape=out_shape,
        input_output_aliases=aliases or {},
        compiler_params=pltpu.CompilerParams(vmem_limit_bytes=VMEM_LIMIT),
        cost_estimate=pl.CostEstimate(flops=flops, bytes_accessed=data, transcendentals=0),
    )


WHOLE = pl.BlockSpec(memory_space=pltpu.VMEM)


def rows_of(ref, c):
    parts = [ref[0, pl.ds(pl.multiple_of(x * 128 + c * 64, 64), 64), :] for x in range(2)]
    return jnp.concatenate(parts, axis=0)


def ask_pack_kernel(at, q_ref, k_ref, v_ref, out_ref):
    other = 1 - at[2]
    out_ref[:, 0:4096] = rows_of(q_ref, other)
    out_ref[:, 4096:4608] = rows_of(k_ref, other)
    out_ref[:, 4608:5120] = rows_of(v_ref, other)


def kv_pack_kernel(at, k_ref, v_ref, *out_refs):
    for s, out_ref in enumerate(out_refs):
        head = pl.ds(pl.multiple_of((at[0] ^ s) * 128, 128), 128)
        out_ref[0:512, :] = k_ref[:, head]
        out_ref[512:1024, :] = v_ref[:, head]


def x_pack_kernel(at, got_ref, q_ref, k_ref, v_ref, keep_ref, send_ref):
    x, c, owner_c = at[1], at[2], at[6]

    def write(ask_q, ask_kv):
        for ref, row_half in ((keep_ref, x), (send_ref, 1 - x)):
            ref[0:64, :] = ask_q(row_half)
            for i in range(4):
                ref[64:96, i * 1024 : (i + 1) * 1024] = ask_kv(i)

    def own_kv(i):
        rows = pl.ds(pl.multiple_of((i // 2) * 128 + c * 64 + (i % 2) * 32, 32), 32)
        return jnp.concatenate([k_ref[0, rows, :], v_ref[0, rows, :]], axis=1)

    @pl.when(owner_c == c)
    def _():
        write(lambda half: q_ref[0, pl.ds(pl.multiple_of(half * 128 + c * 64, 64), 64), :], own_kv)

    @pl.when(owner_c != c)
    def _():
        write(
            lambda half: got_ref[pl.ds(pl.multiple_of(half * 64, 64), 64), 0:4096],
            lambda i: got_ref[i * 32 : (i + 1) * 32, 4096:5120],
        )


def z_pack_kernel(at, keep_ref, got_ref, *out_refs):
    z, x, owner_x = at[0], at[1], at[5]

    def write(ref):
        for s, out_ref in enumerate(out_refs):
            j = z ^ s
            out_ref[0:64, :] = ref[0:64, pl.ds(pl.multiple_of(j * 1024, 1024), 1024)]
            for i in range(4):
                for part in range(2):
                    lanes = pl.ds(pl.multiple_of(i * 1024 + part * 512 + j * 128, 128), 128)
                    out_ref[64:96, i * 256 + part * 128 : i * 256 + (part + 1) * 128] = ref[64:96, lanes]

    @pl.when(owner_x == x)
    def _():
        write(keep_ref)

    @pl.when(owner_x != x)
    def _():
        write(got_ref)


def pick_kernel(at, *refs):
    out_ref = refs[-1]
    for s in range(4):
        @pl.when((at[0] ^ at[4]) == s)
        def _(s=s):
            out_ref[...] = refs[s][...]


def ones_beside(values):
    return jnp.concatenate([values, jnp.ones(values.shape, values.dtype)], axis=1)


def read_kernel(at, own_ref, other_ref, *refs):
    kv_refs, (mine_ref, send_ref, s_ref) = refs[:8], refs[8:]
    z, x, c = at[0], at[1], at[2]
    column = lax.broadcasted_iota(jnp.int32, (1, 512), 1)
    step = pl.program_id(0)
    ask_ref_is_own = step < 2
    lane0 = pl.multiple_of((step % 2) * 512, 512)

    def rows(ref):
        q = ref[0:64, pl.ds(lane0, 512)]
        return jnp.concatenate([q[:, h * 128 : (h + 1) * 128] for h in range(4)], axis=0)

    q = jnp.where(ask_ref_is_own, rows(own_ref), rows(other_ref))
    row_c = jnp.where(ask_ref_is_own, c, 1 - c)
    peak = None
    for i, kv_ref in enumerate(kv_refs):
        xz = (x ^ (i // 4)) * 2 + (z ^ (i % 4)) * 4 + c
        s = jnp.where(column < at[8 + xz], dot_t(q, kv_ref[0:512, :]), masked_score)
        s_ref[:, i * 512 : (i + 1) * 512] = s
        for k in range(4):
            part = s[:, k * 128 : (k + 1) * 128]
            peak = part if peak is None else jnp.maximum(peak, part)
    ask_k = jnp.concatenate([own_ref[64:96, i * 256 : i * 256 + 128] for i in range(4)], axis=0)
    ask_v = jnp.concatenate([own_ref[64:96, i * 256 + 128 : (i + 1) * 256] for i in range(4)], axis=0)
    key_at = lax.broadcasted_iota(jnp.int32, (256, 128), 1)
    key_at = (key_at // 64) * 128 + c * 64 + key_at % 64
    row_at = lax.broadcasted_iota(jnp.int32, (256, 128), 0) % 64 + x * 128 + row_c * 64
    s_self = jnp.where(key_at <= row_at, dot_t(q, ask_k), masked_score)
    peak = jnp.max(jnp.maximum(peak, s_self), axis=1, keepdims=True) * LOG_SCALE
    total = jnp.dot(
        jnp.exp2(s_self * LOG_SCALE - peak).astype(BF16), ones_beside(ask_v), preferred_element_type=F32
    )
    for i, kv_ref in enumerate(kv_refs):
        w = jnp.exp2(s_ref[:, i * 512 : (i + 1) * 512] * LOG_SCALE - peak).astype(BF16)
        total = total + jnp.dot(w, ones_beside(kv_ref[512:1024, :]), preferred_element_type=F32)
    weight = total[:, 128:]
    result = jnp.concatenate([total[:, :128] / weight, peak + jnp.log2(weight)], axis=1)
    at_row = pl.ds(pl.multiple_of((step % 2) * 256, 256), 256)

    @pl.when(ask_ref_is_own)
    def _():
        mine_ref[at_row, :] = result

    @pl.when(jnp.logical_not(ask_ref_is_own))
    def _():
        send_ref[at_row, :] = result


def merge_kernel(at, mine_ref, got_ref, out_ref):
    top = jnp.maximum(mine_ref[:, 128:], got_ref[:, 128:])
    one, two = jnp.exp2(mine_ref[:, 128:] - top), jnp.exp2(got_ref[:, 128:] - top)
    answer = ((one * mine_ref[:, :128] + two * got_ref[:, :128]) / (one + two)).astype(BF16)
    for h in range(8):
        out_ref[:, h * 128 : (h + 1) * 128] = answer[h * 64 : (h + 1) * 64, :]


def project_kernel(at, *refs):
    parts, w_ref, keep_ref, send_ref, sum_ref = refs[:16], refs[16], refs[17], refs[18], refs[19]
    z, x, c, t = at[0], at[1], at[2], at[3]
    for s in range(4):
        w = w_ref[pl.ds(pl.multiple_of((z ^ s) * 1024, 1024), 1024), :]
        a = jnp.concatenate([parts[s * 4 + r][...] for r in range(4)], axis=0)
        product = jnp.dot(a, w, preferred_element_type=F32)
        if s == 0:
            sum_ref[...] = product
        else:
            sum_ref[...] += product
    for r in range(4):
        half, core = x ^ (r // 2), c ^ (r % 2)
        at_row = pl.ds(pl.multiple_of(core * 64, 64), 64)
        quarter = sum_ref[r * 64 : (r + 1) * 64, :]

        @pl.when(half == t)
        def _(quarter=quarter, at_row=at_row):
            keep_ref[at_row, :] = quarter

        @pl.when(half != t)
        def _(quarter=quarter, at_row=at_row):
            send_ref[at_row, :] = quarter.astype(BF16)


def encode_kernel(at, q_ref, k_ref, v_ref, ak_ref, av_ref, *rest):
    o_ref = rest[-1]
    row = lax.broadcasted_iota(jnp.int32, (256, 256), 0)
    column = lax.broadcasted_iota(jnp.int32, (256, 256), 1)
    anchor_len = jnp.where(at[7] > 0, at[8], 0)
    anchor_ok = lax.broadcasted_iota(jnp.int32, (1, 512), 1) < anchor_len
    own_len = at[8 + at[7]]
    anchor_v = ones_beside(av_ref[...])
    own_v = [ones_beside(v_ref[r * 256 : (r + 1) * 256, :]) for r in range(2)]
    for h in range(8):
        lanes = slice(h * 128, (h + 1) * 128)
        for r in range(2):
            here = slice(r * 256, (r + 1) * 256)
            q = q_ref[here, lanes]
            scores = [jnp.where(anchor_ok, dot_t(q, ak_ref[...]), masked_score)]
            values = [anchor_v]
            for b in range(r + 1):
                s = dot_t(q, k_ref[b * 256 : (b + 1) * 256, :])
                scores.append(jnp.where(column <= row, s, masked_score) if b == r else s)
                values.append(own_v[b])
            peak = functools.reduce(jnp.maximum, [s.max(axis=1, keepdims=True) for s in scores]) * LOG_SCALE
            total = 0
            for s, v in zip(scores, values):
                w = jnp.exp2(s * LOG_SCALE - peak).astype(BF16)
                total = total + jnp.dot(w, v, preferred_element_type=F32)
            valid = lax.broadcasted_iota(jnp.int32, (256, 128), 0) + r * 256 < own_len
            o_ref[here, lanes] = jnp.where(valid, total[:, :128] / total[:, 128:], 0.0).astype(BF16)


def anchors(key, value, at):
    z, x, c = at[0], at[1], at[2]

    def send(array, pairs):
        return lax.ppermute(array, "hst", pairs)

    got = send(value, [(0, 1)])
    half = jnp.where(c == 0, key, got)
    got = send(half, [(0, 2), (1, 3)])
    half = jnp.where(x == 0, half, got)
    got = send(half, [(i, i + 8) for i in range(4)])
    half = jnp.where(z == 0, half, got)
    got = send(half, [(i, i + 4) for i in (0, 1, 2, 3, 8, 9, 10, 11)])
    half = jnp.where(z % 2 == 0, half, got)
    got = swap(half, 1)
    return jnp.where(c == 0, half, got), jnp.where(c == 0, got, half)


def body(ctx_query, ctx_key, context_value, lengths, owner, ask_query, ask_key, candidate_value_rows, out_weight):
    host, t = lax.axis_index("hst"), lax.axis_index("tensor")
    own = owner[0]
    at = jnp.concatenate([
        jnp.stack([host // 4, host // 2 % 2, host % 2, t, own // 4, own // 2 % 2, own % 2, host]).astype(jnp.int32),
        lengths,
    ])
    shape = jax.ShapeDtypeStruct

    packed = call(ask_pack_kernel, shape((128, 5120), BF16), [WHOLE] * 3, WHOLE)(
        at, ask_query, ask_key, candidate_value_rows
    )
    got = swap(packed, 1)
    kv = call(kv_pack_kernel, [shape((1024, 128), BF16)] * 4, [WHOLE] * 2, [WHOLE] * 4)(at, ctx_key, context_value)
    kv_z = [kv[0]] + [swap(kv[s], 4 * s) for s in (1, 2, 3)]
    keep, send = call(x_pack_kernel, [shape((96, 4096), BF16)] * 2, [WHOLE] * 4, [WHOLE] * 2)(
        at, got, ask_query, ask_key, candidate_value_rows
    )
    got = swap(send, 2)
    asked = call(z_pack_kernel, [shape((96, 1024), BF16)] * 4, [WHOLE] * 2, [WHOLE] * 4)(at, keep, got)
    asked = [asked[0]] + [swap(asked[s], 4 * s) for s in (1, 2, 3)]
    asked = call(pick_kernel, shape((96, 1024), BF16), [WHOLE] * 4, WHOLE)(at, *asked)
    asked_other = swap(asked, 1)
    kv_x = [swap(part, 2) for part in kv_z]

    anchor_key, anchor_value = anchors(ctx_key, context_value, at)

    mine, send = call(
        read_kernel, [shape((512, 256), F32)] * 2, [WHOLE] * 10, [WHOLE] * 2, grid=(4,),
        scratch=[pltpu.VMEM((256, 4096), F32)], flops=2 * 2 * 1024 * 4096 * 256, data=2**21,
    )(at, asked, asked_other, *kv_z, *kv_x)
    got = swap(send, 1)
    answer = call(merge_kernel, shape((64, 1024), BF16), [WHOLE] * 2, WHOLE)(at, mine, got)

    across = [answer] + [swap(answer, 4 * s) for s in (1, 2, 3)]
    sides = [swap(part, 2) for part in across]
    here = [(across[s], sides[s]) for s in range(4)]
    flat = jnp.stack([part for pair in here for part in pair])
    there = swap(flat, 1)

    ctx_out = None
    for g in range(4):
        block = pl.BlockSpec((512, 1024), lambda i, at, g=g: (0, g))
        head = pl.BlockSpec((512, 128), lambda i, at, g=g: (0, g))
        args = [ctx_query, ctx_key, context_value, anchor_key, anchor_value] + ([] if g == 0 else [ctx_out])
        ctx_out = call(
            encode_kernel, shape((512, 4096), BF16), [block] + [head] * 4 + ([] if g == 0 else [pl.BlockSpec(memory_space=pl.ANY)]),
            block, grid=(1,), aliases={} if g == 0 else {6: 0}, flops=4 * 4096 * 1024 * 256, data=2**21,
        )(at, *args)

    parts = []
    for s in range(4):
        parts += [here[s][0], there[2 * s], here[s][1], there[2 * s + 1]]
    keep, send = call(
        project_kernel, [shape((128, 512), F32), shape((128, 512), BF16)], [WHOLE] * 17, [WHOLE] * 2,
        scratch=[pltpu.VMEM((256, 512), F32)], flops=2 * 256 * 4096 * 512, data=2**22,
    )(at, *parts, out_weight)
    got = lax.ppermute(send, "tensor", [(0, 1), (1, 0)])
    return ctx_out, (keep + got.astype(F32)).astype(BF16)


def solution(mesh):
    placed = (
        P("hst", "tensor"),
        P("hst", "tensor"),
        P("hst", "tensor"),
        P(),
        P(),
        P("hst", None, "tensor"),
        P("hst", None, "tensor"),
        P("hst", None, "tensor"),
        P("tensor", "hst"),
    )
    fits = dict(mesh.shape) == {"hst": 16, "tensor": 2}
    return jax.shard_map(
        body if fits else generic_body,
        mesh=mesh,
        in_specs=placed,
        out_specs=(P("hst", "tensor"), P("tensor", "hst")),
        check_vma=False,
    )
```

```python
import functools
import math

import jax
import jax.numpy as jnp
from jax import lax
from jax.experimental import pallas as pl
from jax.experimental.pallas import tpu as pltpu
from jax.sharding import PartitionSpec as P

HEAD_SIZE = 128
F32 = jnp.float32
BF16 = jnp.bfloat16
LOG_SCALE = math.log2(math.e) / math.sqrt(HEAD_SIZE)


masked_score = -1e30


def broadcast(block, axis, owner):
    block = jnp.where(lax.axis_index(axis) == owner, block, jnp.zeros_like(block))
    return lax.psum(block, axis)


def combined_all(array, axis, combine):
    everything = jax.tree.map(lambda part: lax.all_gather(part, axis), array)
    first = jax.tree.map(lambda part: part[0], everything)

    def hop(k, so_far):
        return combine(so_far, jax.tree.map(lambda part: part[k], everything))

    return lax.fori_loop(1, lax.axis_size(axis), hop, first)


def partial_attend(queries, keys, values, allowed):
    rows = queries.shape[0]
    groups = keys.shape[1] // HEAD_SIZE
    query_heads = queries.reshape(rows, groups, -1, HEAD_SIZE)
    key_heads = keys.reshape(keys.shape[0], groups, HEAD_SIZE)
    value_heads = values.reshape(values.shape[0], groups, HEAD_SIZE)
    scores = jnp.einsum(
        "rkgd,skd->rkgs", query_heads, key_heads, preferred_element_type=jnp.float32
    ) / math.sqrt(HEAD_SIZE)
    scores = jnp.where(allowed[:, None, None, :], scores, masked_score)
    peaks = jnp.max(scores, axis=-1)
    weights = jnp.exp(scores - peaks[..., None]).astype(jnp.bfloat16)
    totals = jnp.sum(weights.astype(jnp.float32), axis=-1)
    outputs = jnp.einsum("rkgs,skd->rkgd", weights, value_heads, preferred_element_type=jnp.float32)
    return (peaks.reshape(rows, -1), totals.reshape(rows, -1), outputs.reshape(rows, -1))


def normalize(outputs, totals):
    rows, heads = totals.shape
    return (outputs.reshape(rows, heads, -1) / totals[..., None]).reshape(rows, -1)


def combine(first_piece, second_piece):
    rows, heads = first_piece[0].shape
    top = jnp.maximum(first_piece[0], second_piece[0])
    scale_one = jnp.exp(first_piece[0] - top)
    scale_two = jnp.exp(second_piece[0] - top)
    totals = scale_one * first_piece[1] + scale_two * second_piece[1]
    outputs = (
        first_piece[2].reshape(rows, heads, -1) * scale_one[..., None]
        + second_piece[2].reshape(rows, heads, -1) * scale_two[..., None]
    )
    return (top, totals, outputs.reshape(rows, -1))


def generic_body(
    ctx_query,
    ctx_key,
    context_value,
    lengths,
    owner,
    ask_query,
    ask_key,
    candidate_value_rows,
    out_weight,
):
    host = lax.axis_index("hst")
    anchor_key, anchor_value = (broadcast(ctx_key, "hst", 0), broadcast(context_value, "hst", 0))
    block_len = ctx_query.shape[0]
    own_len = lengths[host]
    anchor_len = lengths[0]
    keys_all = jnp.concatenate([anchor_key, ctx_key], axis=0)
    values_all = jnp.concatenate([anchor_value, context_value], axis=0)
    rows_each = min(512, block_len)
    columns = jnp.arange(block_len, dtype=jnp.int32)
    row_pos = 0 + jnp.arange(rows_each, dtype=jnp.int32)
    anchor_ok = jnp.broadcast_to(
        (columns[None, :] < anchor_len) & (host > 0), (rows_each, block_len)
    )
    own_ok = (columns[None, :] <= row_pos[:, None]) & (columns[None, :] < own_len)
    allowed = jnp.concatenate([anchor_ok, own_ok], axis=1)
    peaks, totals, outputs = partial_attend(ctx_query, keys_all, values_all, allowed)
    result = jnp.where(row_pos[:, None] < own_len, normalize(outputs, totals), 0.0)
    pieces = result.astype(jnp.bfloat16)
    chosen = owner[0]
    query_rows = ask_query.shape[1]
    query_pos = jnp.arange(query_rows, dtype=jnp.int32)
    causal = query_pos[None, :] <= query_pos[:, None]
    block_ok = jnp.broadcast_to((columns < own_len)[None, :], (query_rows, block_len))
    asked, ask_keys, ask_values = (
        broadcast(ask_query[0], "hst", chosen),
        broadcast(ask_key[0], "hst", chosen),
        broadcast(candidate_value_rows[0], "hst", chosen),
    )
    local = partial_attend(asked, ctx_key, context_value, block_ok)
    pending = partial_attend(asked, ask_keys, ask_values, causal)
    merged = combined_all(local, "hst", combine)
    merged = combine(merged, pending)
    answer = normalize(merged[2], merged[1]).astype(jnp.bfloat16)
    projected = jnp.dot(answer, out_weight, preferred_element_type=jnp.float32)
    layer_out = lax.psum_scatter(
        projected.astype(jnp.bfloat16), "tensor", scatter_dimension=0, tiled=True
    )
    return (pieces, layer_out)


def dot_t(a, b):
    return lax.dot_general(a, b, (((1,), (1,)), ((), ())), preferred_element_type=F32)


def swap(array, bit):
    return lax.ppermute(array, "hst", [(i, i ^ bit) for i in range(16)])


def place():
    host = lax.axis_index("hst")
    return host // 4, host // 2 % 2, host % 2


def call(
    kernel, out_shape, in_specs, out_specs, args, scalars=(), after=(), grid=(), scratch=(), flops=0, data=0, aliases=None, vmem=8
):
    n, m = len(scalars), len(after)

    def body(*refs):
        kernel(*refs[:n], *refs[n + m :])

    return pl.pallas_call(
        body,
        grid_spec=pltpu.PrefetchScalarGridSpec(
            num_scalar_prefetch=n,
            grid=grid,
            in_specs=[pl.BlockSpec(memory_space=pl.ANY)] * m + in_specs,
            out_specs=out_specs,
            scratch_shapes=list(scratch),
        ),
        out_shape=out_shape,
        input_output_aliases={n + m + i: o for i, o in (aliases or {}).items()},
        compiler_params=pltpu.CompilerParams(vmem_limit_bytes=vmem * 2**20),
        cost_estimate=pl.CostEstimate(flops=flops, bytes_accessed=data, transcendentals=0),
    )(*scalars, *after, *args)


shape = jax.ShapeDtypeStruct
WHOLE = pl.BlockSpec(memory_space=pltpu.VMEM)
ANY = pl.BlockSpec(memory_space=pl.ANY)


def in_hbm(*arrays):
    return [pltpu.with_memory_space_constraint(array, pltpu.HBM) for array in arrays]


def in_vmem(*arrays):
    return [pltpu.with_memory_space_constraint(array, pltpu.VMEM) for array in arrays]


def lanes(start, size):
    return pl.ds(pl.multiple_of(start, 128), size)


def rows(start, size):
    return pl.ds(pl.multiple_of(start, 64), size)


def copy_all(pairs, sems):
    copies = [pltpu.make_async_copy(a, b, sems.at[i]) for i, (a, b) in enumerate(pairs)]
    for copy in copies:
        copy.start()
    for copy in copies:
        copy.wait()


def ask_pack_kernel(q_ref, k_ref, v_ref, out_ref, sems):
    _, _, c = place()
    pairs = []
    for x in range(2):
        here, there = rows(x * 128 + (1 - c) * 64, 64), slice(x * 64, (x + 1) * 64)
        pairs += [
            (q_ref.at[0, here], out_ref.at[there, 0:4096]),
            (k_ref.at[0, here], out_ref.at[there, 4096:4608]),
            (v_ref.at[0, here], out_ref.at[there, 4608:5120]),
        ]
    copy_all(pairs, sems)


def kv_pack_kernel(k_ref, v_ref, *refs):
    z, _, _ = place()
    pairs = []
    for s, out_ref in enumerate(refs[:4]):
        head = lanes((z ^ s) * 128, 128)
        pairs += [(k_ref.at[:, head], out_ref.at[0:512]), (v_ref.at[:, head], out_ref.at[512:1024])]
    copy_all(pairs, refs[4])


def x_pack_kernel(owner, got_ref, q_ref, k_ref, v_ref, send_ref, sems):
    _, x, c = place()
    owner_c = owner[0] % 2

    @pl.when(owner_c == c)
    def _():
        pairs = [(q_ref.at[0, rows((1 - x) * 128 + c * 64, 64)], send_ref.at[:, 0:4096])]
        for i in range(2):
            here, to = rows(i * 128 + c * 64, 64), 4096 + i * 1024
            pairs += [
                (k_ref.at[0, here], send_ref.at[:, to : to + 512]),
                (v_ref.at[0, here], send_ref.at[:, to + 512 : to + 1024]),
            ]
        copy_all(pairs, sems)

    @pl.when(owner_c != c)
    def _():
        send_ref[:, 0:4096] = got_ref[rows((1 - x) * 64, 64), 0:4096]
        for i in range(2):
            to = 4096 + i * 1024
            send_ref[:, to : to + 1024] = got_ref[i * 64 : (i + 1) * 64, 4096:5120]


def z_pack_kernel(owner, c_ref, x_ref, q_ref, k_ref, v_ref, *refs):
    z, x, c = place()
    outs, sems = refs[:4], refs[4]
    owner_c, owner_x = owner[0] % 2, owner[0] // 2 % 2

    @pl.when(owner_x != x)
    def _():
        for s, out_ref in enumerate(outs):
            j = z ^ s
            out_ref[:, 0:1024] = x_ref[:, lanes(j * 1024, 1024)]
            for i in range(4):
                out_ref[:, 1024 + i * 128 : 1152 + i * 128] = x_ref[:, lanes(4096 + i * 512 + j * 128, 128)]

    @pl.when((owner_x == x) & (owner_c == c))
    def _():
        pairs = []
        for s, out_ref in enumerate(outs):
            j = z ^ s
            pairs.append((q_ref.at[0, rows(x * 128 + c * 64, 64), lanes(j * 1024, 1024)], out_ref.at[:, 0:1024]))
            for i in range(4):
                part = (k_ref, v_ref)[i % 2].at[0, rows(i // 2 * 128 + c * 64, 64), lanes(j * 128, 128)]
                pairs.append((part, out_ref.at[:, 1024 + i * 128 : 1152 + i * 128]))
        copy_all(pairs, sems)

    @pl.when((owner_x == x) & (owner_c != c))
    def _():
        for s, out_ref in enumerate(outs):
            j = z ^ s
            out_ref[:, 0:1024] = c_ref[rows(x * 64, 64), lanes(j * 1024, 1024)]
            for i in range(4):
                part = c_ref[i // 2 * 64 : (i // 2 + 1) * 64, lanes(4096 + i % 2 * 512 + j * 128, 128)]
                out_ref[:, 1024 + i * 128 : 1152 + i * 128] = part


def ones_beside(values):
    return jnp.concatenate([values, jnp.ones(values.shape, values.dtype)], axis=1)


def read_kernel(owner, lengths, *refs):
    asked, (own_kv, other_kv), parts, out_ref, q_ref = refs[:4], refs[4:6], refs[6:22], refs[22], refs[23]
    z, x, c = place()
    step = pl.program_id(0)
    at = z ^ (owner[0] // 4)
    for s in range(4):

        @pl.when(at == s)
        def _(s=s):
            for h in range(4):
                q_ref[h * 64 : (h + 1) * 64, :] = asked[s][:, lanes(step * 512 + h * 128, 128)]

    q = q_ref[...]
    column = lax.broadcasted_iota(jnp.int32, (1, 512), 1)
    found = []

    def add(scores, values):
        peak = row_max(scores)
        total = 0
        for s, v in zip(scores, values):
            total = total + jnp.dot(weights(s, peak), ones_beside(v), preferred_element_type=F32)
        found.append((peak, total))

    for pair in range(8):
        scores, values = [], []
        for i in (2 * pair, 2 * pair + 1):
            block = ((z ^ (i % 4)) * 2 + (x ^ (i // 4 % 2))) * 2 + (c ^ (i // 8))
            scores.append(jnp.where(column < lengths[block], dot_t(q, parts[i][0:512, :]), masked_score))
            values.append(parts[i][512:1024, :])
        add(scores, values)
    row_at = lax.broadcasted_iota(jnp.int32, (256, 64), 0) % 64 + x * 128 + c * 64
    column = lax.broadcasted_iota(jnp.int32, (256, 64), 1)
    scores, values = [], []
    for ref, core in ((own_kv, c), (other_kv, 1 - c)):
        for i in range(2):
            s = dot_t(q, ref[:, i * 256 : i * 256 + 128])
            scores.append(jnp.where(column + i * 128 + core * 64 <= row_at, s, masked_score))
            values.append(ref[:, i * 256 + 128 : (i + 1) * 256])
    add([jnp.concatenate(scores, axis=1)], [jnp.concatenate(values, axis=0)])
    top = functools.reduce(jnp.maximum, [peak for peak, _ in found])
    scales = [jnp.exp2(peak - top) for peak, _ in found]
    sums = sum(scale * part[:, :128] for scale, (_, part) in zip(scales, found))
    total = sum(scale * part[:, 128:] for scale, (_, part) in zip(scales, found))
    answer = (sums / total).astype(BF16)
    for h in range(4):
        out_ref[:, h * 128 : (h + 1) * 128] = answer[h * 64 : (h + 1) * 64, :]


def project_kernel(*refs):
    near, near_far, side, side_far, w_ref, keep_ref, send_ref, sum_ref = refs
    z, x, c = place()
    t = lax.axis_index("tensor")
    for s in range(4):
        w = w_ref[pl.ds(pl.multiple_of((z ^ s) * 1024, 1024), 1024), :]
        across = [(near, s), (near_far, s), (near, 4) if s == 0 else (side, s - 1), (near_far, 4) if s == 0 else (side_far, s - 1)]
        a = jnp.concatenate([ref[i] for ref, i in across], axis=0)
        product = jnp.dot(a, w, preferred_element_type=F32)
        if s == 0:
            sum_ref[...] = product
        else:
            sum_ref[...] += product
    for r in range(4):
        half, core = x ^ (r // 2), c ^ (r % 2)
        at_row = rows(core * 64, 64)
        quarter = sum_ref[r * 64 : (r + 1) * 64, :]

        @pl.when(half == t)
        def _(quarter=quarter, at_row=at_row):
            keep_ref[at_row, :] = quarter

        @pl.when(half != t)
        def _(quarter=quarter, at_row=at_row):
            send_ref[at_row, :] = quarter.astype(BF16)


def row_max(scores):
    tiles = [s[:, i : i + 128] for s in scores for i in range(0, s.shape[1], 128)]
    peak = jnp.max(functools.reduce(jnp.maximum, tiles), axis=1, keepdims=True)
    return jnp.broadcast_to(peak * LOG_SCALE, (scores[0].shape[0], 128))


def weights(s, peak):
    tiles = [jnp.exp2(s[:, i : i + 128] * LOG_SCALE - peak).astype(BF16) for i in range(0, s.shape[1], 128)]
    return jnp.concatenate(tiles, axis=1)


def own_kernel(q_ref, k_ref, v_ref, *rest):
    o_ref, lse_ref = rest[-2:]
    row = lax.broadcasted_iota(jnp.int32, (256, 256), 0)
    column = lax.broadcasted_iota(jnp.int32, (256, 256), 1)
    lane = lax.broadcasted_iota(jnp.int32, (256, 128), 1)

    def half(r):
        own_v = [ones_beside(v_ref[b * 256 : (b + 1) * 256, :]) for b in range(r + 1)]
        found = jnp.zeros((256, 128), F32)
        for h in range(8):
            q = q_ref[:, h * 128 : (h + 1) * 128]
            scores = []
            for b in range(r + 1):
                s = dot_t(q, k_ref[b * 256 : (b + 1) * 256, :])
                scores.append(jnp.where(column <= row, s, masked_score) if b == r else s)
            peak = row_max(scores)
            total = 0
            for b in range(r + 1):
                total = total + jnp.dot(weights(scores[b], peak), own_v[b], preferred_element_type=F32)
            o_ref[:, h * 128 : (h + 1) * 128] = (total[:, :128] / total[:, 128:]).astype(BF16)
            found = jnp.where(lane == h, peak + jnp.log2(total[:, 128:]), found)
        lse_ref[...] = found

    @pl.when(pl.program_id(0) == 0)
    def _():
        half(0)

    @pl.when(pl.program_id(0) == 1)
    def _():
        half(1)


def anchor_kernel(lengths, q_ref, own_ref, lse_ref, near_k_ref, near_v_ref, far_k_ref, far_v_ref, *rest):
    o_ref = rest[-1]
    host = lax.axis_index("hst")
    anchor_len = jnp.where(host > 0, lengths[0], 0)
    own_len = lengths[host] - pl.program_id(0) * 256
    _, x, _ = place()
    column = lax.broadcasted_iota(jnp.int32, (1, 256), 1)
    parts = [
        (near_k_ref, column + x * 256 < anchor_len, ones_beside(near_v_ref[...])),
        (far_k_ref, column + (1 - x) * 256 < anchor_len, ones_beside(far_v_ref[...])),
    ]
    valid = lax.broadcasted_iota(jnp.int32, (256, 128), 0) < own_len
    for h in range(8):
        at = slice(h * 128, (h + 1) * 128)
        scores = [jnp.where(ok, dot_t(q_ref[:, at], k_ref[...]), masked_score) for k_ref, ok, _ in parts]
        lse = jnp.broadcast_to(lse_ref[:, h : h + 1], (256, 128))
        peak = jnp.maximum(row_max(scores), lse)
        total = 0
        for s, (_, _, values) in zip(scores, parts):
            total = total + jnp.dot(weights(s, peak), values, preferred_element_type=F32)
        own = jnp.exp2(lse - peak)
        result = (total[:, :128] + own * own_ref[:, at].astype(F32)) / (total[:, 128:] + own)
        o_ref[:, at] = jnp.where(valid, result, 0.0).astype(BF16)


def body(ctx_query, ctx_key, context_value, lengths, owner, ask_query, ask_key, candidate_value_rows, out_weight):
    z, x, c = place()
    ask = [ask_query, ask_key, candidate_value_rows]
    dma = pltpu.SemaphoreType.DMA

    def send(array, pairs):
        return lax.ppermute(array, "hst", pairs)

    def after(array, *others):
        return lax.optimization_barrier((array, *others))[0]

    own_out, lse = None, []

    def own(g, *others):
        nonlocal own_out
        block = pl.BlockSpec((256, 1024), lambda i, g=g: (i, g))
        head = pl.BlockSpec((512, 128), lambda i, g=g: (0, g))
        own_out, found = call(
            own_kernel, [pltpu.HBM((512, 4096), BF16), pltpu.HBM((512, 128), F32)],
            [block, head, head] + ([] if g == 0 else [ANY]),
            [block, pl.BlockSpec((256, 128), lambda i: (i, 0))],
            in_hbm(ctx_query, ctx_key, context_value) + ([] if g == 0 else in_hbm(own_out)),
            after=others, grid=(2,), aliases={} if g == 0 else {3: 0}, flops=4 * 4096 * 768 * 256, data=2**21, vmem=16,
        )
        lse.append(found)
        return found

    ctx_out = None

    def encode(g, *others):
        nonlocal ctx_out
        block = pl.BlockSpec((256, 1024), lambda i, _, g=g: (i, g))
        head = pl.BlockSpec((256, 128), lambda i, _, g=g: (0, g))
        ctx_out = call(
            anchor_kernel, pltpu.HBM((512, 4096), BF16),
            [block, block, pl.BlockSpec((256, 128), lambda i, _: (i, 0))] + [head] * 4
            + ([] if g == 0 else [ANY]),
            block,
            in_hbm(ctx_query, own_out, lse[g]) + anchor + ([] if g == 0 else in_hbm(ctx_out)),
            scalars=[lengths], after=others, grid=(2,), aliases={} if g == 0 else {7: 0},
            flops=4 * 4096 * 512 * 256, data=2**21, vmem=16,
        )
        return ctx_out

    kv = call(
        kv_pack_kernel, [pltpu.HBM((1024, 128), BF16)] + [shape((1024, 128), BF16)] * 3, [ANY] * 2, [WHOLE] * 4,
        in_hbm(ctx_key, context_value), scratch=[dma((8,))],
    )
    packed = call(
        ask_pack_kernel, shape((128, 5120), BF16), [ANY] * 3, WHOLE, in_hbm(*ask), after=[kv[0]], scratch=[dma((6,))]
    )
    got_c = swap(packed, 1)
    kv_z = [kv[0]] + [swap(kv[s], 4 * s) for s in (1, 2, 3)]
    sent = call(
        x_pack_kernel, shape((64, 6144), BF16), [WHOLE] + [ANY] * 3, WHOLE, in_vmem(got_c) + in_hbm(*ask),
        scalars=[owner], scratch=[dma((5,))],
    )
    got_x = swap(sent, 2)

    whole = jnp.where(c == 0, ctx_key, send(after(context_value, packed), [(0, 1)]))
    got = send(after(whole[256:], sent), [(0, 2), (1, 3)])
    quarter = jnp.where(x == 0, whole[:256], got)
    tick = own(0, sent)
    got = send(after(quarter, tick), [(i, i + 8) for i in range(4)])
    quarter = jnp.where(z == 0, quarter, got)
    own(1, kv_z[1])
    tick = own(2, kv_z[2])
    parts = call(
        z_pack_kernel, [pltpu.HBM((64, 1536), BF16)] + [shape((64, 1536), BF16)] * 3, [WHOLE] * 2 + [ANY] * 3, [WHOLE] * 4,
        in_vmem(got_c, got_x) + in_hbm(*ask), scalars=[owner], after=[tick], scratch=[dma((20,))],
    )
    asked = [parts[0]] + [swap(parts[s], 4 * s) for s in (1, 2, 3)]
    tick = own(3, parts[0])
    kv_x = [swap(after(part, parts[0]), 2) for part in kv_z]
    kv_near = kv_z + kv_x
    kv_far = [swap(after(part, parts[0]), 1) for part in kv_near]

    level = z ^ (owner[0] // 4)
    own_kv = asked[0][:, 1024:]
    for s in (1, 2, 3):
        own_kv = jnp.where(level == s, asked[s][:, 1024:], own_kv)
    other_kv = swap(own_kv, 1)
    answer = call(
        read_kernel, shape((64, 1024), BF16), [WHOLE] * 22, pl.BlockSpec((64, 512), lambda i, *_: (0, i)),
        [asked[0]] + in_vmem(*asked[1:], own_kv, other_kv) + kv_near[:1] + in_vmem(*kv_near[1:], *kv_far),
        scalars=[owner, lengths], grid=(2,),
        scratch=[pltpu.VMEM((256, 128), BF16)], flops=4 * 512 * 8192 * 256, data=2**22, vmem=20,
    )

    got = send(after(quarter, tick), [(i, i + 4) for i in (0, 1, 2, 3, 8, 9, 10, 11)])
    near = jnp.where(z % 2 == 0, quarter, got)
    far = swap(near, 2)
    anchor = []
    for half in (near, far):
        got = swap(half, 1)
        anchor += [jnp.where(c == 0, half, got), jnp.where(c == 0, got, half)]

    across = [swap(answer, 4 * s) for s in (1, 2, 3)]
    side = swap(answer, 2)
    encode(0, answer)
    tick = encode(1)
    across = [after(part, tick) for part in across]
    sides = [swap(part, 2) for part in across]
    near = jnp.stack([answer] + across + [after(side, tick)])
    near_far = swap(near, 1)
    tick = encode(2)
    side = jnp.stack([after(part, tick) for part in sides])
    side_far = swap(side, 1)
    keep, sent = call(
        project_kernel, [shape((128, 512), F32), shape((128, 512), BF16)], [WHOLE] * 5, [WHOLE] * 2,
        in_vmem(near, near_far, side, side_far, out_weight), scratch=[pltpu.VMEM((256, 512), F32)],
        flops=2 * 256 * 4096 * 512, data=2**22, vmem=16,
    )
    got = lax.ppermute(sent, "tensor", [(0, 1), (1, 0)])
    tick = encode(3, sent)
    return ctx_out, (keep + after(got, tick).astype(F32)).astype(BF16)


def solution(mesh):
    placed = (
        P("hst", "tensor"),
        P("hst", "tensor"),
        P("hst", "tensor"),
        P(),
        P(),
        P("hst", None, "tensor"),
        P("hst", None, "tensor"),
        P("hst", None, "tensor"),
        P("tensor", "hst"),
    )
    fits = dict(mesh.shape) == {"hst": 16, "tensor": 2}
    return jax.shard_map(
        body if fits else generic_body,
        mesh=mesh,
        in_specs=placed,
        out_specs=(P("hst", "tensor"), P("tensor", "hst")),
        check_vma=False,
    )
```

```python
import functools
import math

import jax
import jax.numpy as jnp
from jax import lax
from jax.experimental import pallas as pl
from jax.experimental.pallas import tpu as pltpu
from jax.sharding import PartitionSpec as P

HEAD_SIZE = 128
F32 = jnp.float32
BF16 = jnp.bfloat16
LOG_SCALE = math.log2(math.e) / math.sqrt(HEAD_SIZE)


masked_score = -1e30


def broadcast(block, axis, owner):
    block = jnp.where(lax.axis_index(axis) == owner, block, jnp.zeros_like(block))
    return lax.psum(block, axis)


def combined_all(array, axis, combine):
    everything = jax.tree.map(lambda part: lax.all_gather(part, axis), array)
    first = jax.tree.map(lambda part: part[0], everything)

    def hop(k, so_far):
        return combine(so_far, jax.tree.map(lambda part: part[k], everything))

    return lax.fori_loop(1, lax.axis_size(axis), hop, first)


def partial_attend(queries, keys, values, allowed):
    rows = queries.shape[0]
    groups = keys.shape[1] // HEAD_SIZE
    query_heads = queries.reshape(rows, groups, -1, HEAD_SIZE)
    key_heads = keys.reshape(keys.shape[0], groups, HEAD_SIZE)
    value_heads = values.reshape(values.shape[0], groups, HEAD_SIZE)
    scores = jnp.einsum(
        "rkgd,skd->rkgs", query_heads, key_heads, preferred_element_type=jnp.float32
    ) / math.sqrt(HEAD_SIZE)
    scores = jnp.where(allowed[:, None, None, :], scores, masked_score)
    peaks = jnp.max(scores, axis=-1)
    weights = jnp.exp(scores - peaks[..., None]).astype(jnp.bfloat16)
    totals = jnp.sum(weights.astype(jnp.float32), axis=-1)
    outputs = jnp.einsum("rkgs,skd->rkgd", weights, value_heads, preferred_element_type=jnp.float32)
    return (peaks.reshape(rows, -1), totals.reshape(rows, -1), outputs.reshape(rows, -1))


def normalize(outputs, totals):
    rows, heads = totals.shape
    return (outputs.reshape(rows, heads, -1) / totals[..., None]).reshape(rows, -1)


def combine(first_piece, second_piece):
    rows, heads = first_piece[0].shape
    top = jnp.maximum(first_piece[0], second_piece[0])
    scale_one = jnp.exp(first_piece[0] - top)
    scale_two = jnp.exp(second_piece[0] - top)
    totals = scale_one * first_piece[1] + scale_two * second_piece[1]
    outputs = (
        first_piece[2].reshape(rows, heads, -1) * scale_one[..., None]
        + second_piece[2].reshape(rows, heads, -1) * scale_two[..., None]
    )
    return (top, totals, outputs.reshape(rows, -1))


def generic_body(
    ctx_query,
    ctx_key,
    context_value,
    lengths,
    owner,
    ask_query,
    ask_key,
    candidate_value_rows,
    out_weight,
):
    host = lax.axis_index("hst")
    anchor_key, anchor_value = (broadcast(ctx_key, "hst", 0), broadcast(context_value, "hst", 0))
    block_len = ctx_query.shape[0]
    own_len = lengths[host]
    anchor_len = lengths[0]
    keys_all = jnp.concatenate([anchor_key, ctx_key], axis=0)
    values_all = jnp.concatenate([anchor_value, context_value], axis=0)
    rows_each = min(512, block_len)
    columns = jnp.arange(block_len, dtype=jnp.int32)
    row_pos = 0 + jnp.arange(rows_each, dtype=jnp.int32)
    anchor_ok = jnp.broadcast_to(
        (columns[None, :] < anchor_len) & (host > 0), (rows_each, block_len)
    )
    own_ok = (columns[None, :] <= row_pos[:, None]) & (columns[None, :] < own_len)
    allowed = jnp.concatenate([anchor_ok, own_ok], axis=1)
    peaks, totals, outputs = partial_attend(ctx_query, keys_all, values_all, allowed)
    result = jnp.where(row_pos[:, None] < own_len, normalize(outputs, totals), 0.0)
    pieces = result.astype(jnp.bfloat16)
    chosen = owner[0]
    query_rows = ask_query.shape[1]
    query_pos = jnp.arange(query_rows, dtype=jnp.int32)
    causal = query_pos[None, :] <= query_pos[:, None]
    block_ok = jnp.broadcast_to((columns < own_len)[None, :], (query_rows, block_len))
    asked, ask_keys, ask_values = (
        broadcast(ask_query[0], "hst", chosen),
        broadcast(ask_key[0], "hst", chosen),
        broadcast(candidate_value_rows[0], "hst", chosen),
    )
    local = partial_attend(asked, ctx_key, context_value, block_ok)
    pending = partial_attend(asked, ask_keys, ask_values, causal)
    merged = combined_all(local, "hst", combine)
    merged = combine(merged, pending)
    answer = normalize(merged[2], merged[1]).astype(jnp.bfloat16)
    projected = jnp.dot(answer, out_weight, preferred_element_type=jnp.float32)
    layer_out = lax.psum_scatter(
        projected.astype(jnp.bfloat16), "tensor", scatter_dimension=0, tiled=True
    )
    return (pieces, layer_out)


def dot_t(a, b):
    return lax.dot_general(a, b, (((1,), (1,)), ((), ())), preferred_element_type=F32)


def swap(array, bit):
    return lax.ppermute(array, "hst", [(i, i ^ bit) for i in range(16)])


def place():
    host = lax.axis_index("hst")
    return host // 4, host // 2 % 2, host % 2


def call(
    kernel, out_shape, in_specs, out_specs, args, scalars=(), after=(), grid=(), scratch=(), flops=0, data=0, aliases=None, vmem=8
):
    n, m = len(scalars), len(after)

    def body(*refs):
        kernel(*refs[:n], *refs[n + m :])

    return pl.pallas_call(
        body,
        grid_spec=pltpu.PrefetchScalarGridSpec(
            num_scalar_prefetch=n,
            grid=grid,
            in_specs=[pl.BlockSpec(memory_space=pl.ANY)] * m + in_specs,
            out_specs=out_specs,
            scratch_shapes=list(scratch),
        ),
        out_shape=out_shape,
        input_output_aliases={n + m + i: o for i, o in (aliases or {}).items()},
        compiler_params=pltpu.CompilerParams(vmem_limit_bytes=vmem * 2**20),
        cost_estimate=pl.CostEstimate(flops=flops, bytes_accessed=data, transcendentals=0),
    )(*scalars, *after, *args)


shape = jax.ShapeDtypeStruct
WHOLE = pl.BlockSpec(memory_space=pltpu.VMEM)
ANY = pl.BlockSpec(memory_space=pl.ANY)


def in_hbm(*arrays):
    return [pltpu.with_memory_space_constraint(array, pltpu.HBM) for array in arrays]


def in_vmem(*arrays):
    return [pltpu.with_memory_space_constraint(array, pltpu.VMEM) for array in arrays]


def lanes(start, size):
    return pl.ds(pl.multiple_of(start, 128), size)


def rows(start, size):
    return pl.ds(pl.multiple_of(start, 64), size)


def copy_all(pairs, sems):
    copies = [pltpu.make_async_copy(a, b, sems.at[i]) for i, (a, b) in enumerate(pairs)]
    for copy in copies:
        copy.start()
    for copy in copies:
        copy.wait()


def ask_pack_kernel(q_ref, k_ref, v_ref, out_ref, sems):
    _, _, c = place()
    pairs = []
    for x in range(2):
        here, there = rows(x * 128 + (1 - c) * 64, 64), slice(x * 64, (x + 1) * 64)
        pairs += [
            (q_ref.at[0, here], out_ref.at[there, 0:4096]),
            (k_ref.at[0, here], out_ref.at[there, 4096:4608]),
            (v_ref.at[0, here], out_ref.at[there, 4608:5120]),
        ]
    copy_all(pairs, sems)


def kv_pack_kernel(k_ref, v_ref, *refs):
    z, _, _ = place()
    sems, pairs = refs[6], []
    for s, out_ref in enumerate(refs[:4]):
        head = lanes((z ^ s) * 128, 128)
        pairs += [(k_ref.at[:, head], out_ref.at[0:512]), (v_ref.at[:, head], out_ref.at[512:1024])]
    for i, out_ref in enumerate(refs[4:6]):
        here = slice(i * 256, (i + 1) * 256)
        pairs += [(k_ref.at[here], out_ref.at[0:256]), (v_ref.at[here], out_ref.at[256:512])]
    copy_all(pairs, sems)


def x_pack_kernel(owner, got_ref, q_ref, k_ref, v_ref, send_ref, sems):
    _, x, c = place()
    owner_c = owner[0] % 2

    @pl.when(owner_c == c)
    def _():
        pairs = [(q_ref.at[0, rows((1 - x) * 128 + c * 64, 64)], send_ref.at[:, 0:4096])]
        for i in range(2):
            here, to = rows(i * 128 + c * 64, 64), 4096 + i * 1024
            pairs += [
                (k_ref.at[0, here], send_ref.at[:, to : to + 512]),
                (v_ref.at[0, here], send_ref.at[:, to + 512 : to + 1024]),
            ]
        copy_all(pairs, sems)

    @pl.when(owner_c != c)
    def _():
        pairs = [(got_ref.at[rows((1 - x) * 64, 64), 0:4096], send_ref.at[:, 0:4096])]
        for i in range(2):
            to = 4096 + i * 1024
            pairs += [(got_ref.at[i * 64 : (i + 1) * 64, 4096:5120], send_ref.at[:, to : to + 1024])]
        copy_all(pairs, sems)


def z_pack_kernel(owner, c_ref, x_ref, q_ref, k_ref, v_ref, *refs):
    z, x, c = place()
    outs, sems = refs[:4], refs[4]
    owner_c, owner_x = owner[0] % 2, owner[0] // 2 % 2

    @pl.when(owner_x != x)
    def _():
        for s, out_ref in enumerate(outs):
            j = z ^ s
            out_ref[:, 0:1024] = x_ref[:, lanes(j * 1024, 1024)]
            for i in range(4):
                out_ref[:, 1024 + i * 128 : 1152 + i * 128] = x_ref[:, lanes(4096 + i * 512 + j * 128, 128)]

    @pl.when((owner_x == x) & (owner_c == c))
    def _():
        pairs = []
        for s, out_ref in enumerate(outs):
            j = z ^ s
            pairs.append((q_ref.at[0, rows(x * 128 + c * 64, 64), lanes(j * 1024, 1024)], out_ref.at[:, 0:1024]))
            for i in range(4):
                part = (k_ref, v_ref)[i % 2].at[0, rows(i // 2 * 128 + c * 64, 64), lanes(j * 128, 128)]
                pairs.append((part, out_ref.at[:, 1024 + i * 128 : 1152 + i * 128]))
        copy_all(pairs, sems)

    @pl.when((owner_x == x) & (owner_c != c))
    def _():
        pairs = []
        for s, out_ref in enumerate(outs):
            j = z ^ s
            pairs.append((c_ref.at[rows(x * 64, 64), lanes(j * 1024, 1024)], out_ref.at[:, 0:1024]))
            for i in range(4):
                part = c_ref.at[i // 2 * 64 : (i // 2 + 1) * 64, lanes(4096 + i % 2 * 512 + j * 128, 128)]
                pairs.append((part, out_ref.at[:, 1024 + i * 128 : 1152 + i * 128]))
        copy_all(pairs, sems)


def ones_beside(values):
    return jnp.concatenate([values, jnp.ones(values.shape, values.dtype)], axis=1)


def read_kernel(owner, lengths, *refs):
    asked, (own_kv, other_kv), pairs, (out_ref, q_ref) = refs[:4], refs[4:6], refs[6:14], refs[14:]
    z, x, c = place()
    step = pl.program_id(0)
    at = z ^ (owner[0] // 4)
    for s in range(4):

        @pl.when(at == s)
        def _(s=s):
            for h in range(4):
                q_ref[h * 64 : (h + 1) * 64, :] = asked[s][:, lanes(step * 512 + h * 128, 128)]

    q = q_ref[...]
    column = lax.broadcasted_iota(jnp.int32, (1, 512), 1)
    found = []

    def add(scores, values):
        peak = row_max(scores)
        total = 0
        for s, v in zip(scores, values):
            total = total + jnp.dot(weights(s, peak), ones_beside(v), preferred_element_type=F32)
        found.append((peak, total))

    for pair, ref in enumerate(pairs):
        scores, values = [], []
        for i in range(2):
            block = ((z ^ (pair % 2 * 2 + i)) * 2 + (x ^ (pair // 2 % 2))) * 2 + (c ^ (pair // 4))
            k, v = ref[i * 1024 : i * 1024 + 512, :], ref[i * 1024 + 512 : (i + 1) * 1024, :]
            scores.append(jnp.where(column < lengths[block], dot_t(q, k), masked_score))
            values.append(v)
        add(scores, values)
    row_at = lax.broadcasted_iota(jnp.int32, (256, 64), 0) % 64 + x * 128 + c * 64
    column = lax.broadcasted_iota(jnp.int32, (256, 64), 1)
    scores, values = [], []
    for ref, core in ((own_kv, c), (other_kv, 1 - c)):
        for i in range(2):
            s = dot_t(q, ref[:, i * 256 : i * 256 + 128])
            scores.append(jnp.where(column + i * 128 + core * 64 <= row_at, s, masked_score))
            values.append(ref[:, i * 256 + 128 : (i + 1) * 256])
    add([jnp.concatenate(scores, axis=1)], [jnp.concatenate(values, axis=0)])
    top = functools.reduce(jnp.maximum, [peak for peak, _ in found])
    scales = [jnp.exp2(peak - top) for peak, _ in found]
    sums = sum(scale * part[:, :128] for scale, (_, part) in zip(scales, found))
    total = sum(scale * part[:, 128:] for scale, (_, part) in zip(scales, found))
    answer = (sums / total).astype(BF16)
    for h in range(4):
        out_ref[:, h * 128 : (h + 1) * 128] = answer[h * 64 : (h + 1) * 64, :]


def project_kernel(*refs):
    near, near_far, side, side_far, w_ref, keep_ref, send_ref, sum_ref = refs
    z, x, c = place()
    t = lax.axis_index("tensor")
    for s in range(4):
        w = w_ref[pl.ds(pl.multiple_of((z ^ s) * 1024, 1024), 1024), :]
        across = [(near, s), (near_far, s), (near, 4) if s == 0 else (side, s - 1), (near_far, 4) if s == 0 else (side_far, s - 1)]
        a = jnp.concatenate([ref[i] for ref, i in across], axis=0)
        product = jnp.dot(a, w, preferred_element_type=F32)
        if s == 0:
            sum_ref[...] = product
        else:
            sum_ref[...] += product
    for r in range(4):
        half, core = x ^ (r // 2), c ^ (r % 2)
        at_row = rows(core * 64, 64)
        quarter = sum_ref[r * 64 : (r + 1) * 64, :]

        @pl.when(half == t)
        def _(quarter=quarter, at_row=at_row):
            keep_ref[at_row, :] = quarter

        @pl.when(half != t)
        def _(quarter=quarter, at_row=at_row):
            send_ref[at_row, :] = quarter.astype(BF16)


def row_max(scores):
    tiles = [s[:, i : i + 128] for s in scores for i in range(0, s.shape[1], 128)]
    peak = jnp.max(functools.reduce(jnp.maximum, tiles), axis=1, keepdims=True)
    return jnp.broadcast_to(peak * LOG_SCALE, (scores[0].shape[0], 128))


def weights(s, peak):
    tiles = [jnp.exp2(s[:, i : i + 128] * LOG_SCALE - peak).astype(BF16) for i in range(0, s.shape[1], 128)]
    return jnp.concatenate(tiles, axis=1)


def own_kernel(q_ref, k_ref, v_ref, *rest):
    o_ref, lse_ref = rest[-2:]
    row = lax.broadcasted_iota(jnp.int32, (256, 256), 0)
    column = lax.broadcasted_iota(jnp.int32, (256, 256), 1)
    lane = lax.broadcasted_iota(jnp.int32, (256, 128), 1)

    def half(r):
        own_v = [ones_beside(v_ref[b * 256 : (b + 1) * 256, :]) for b in range(r + 1)]
        found = jnp.zeros((256, 128), F32)
        for h in range(8):
            q = q_ref[:, h * 128 : (h + 1) * 128]
            scores = []
            for b in range(r + 1):
                s = dot_t(q, k_ref[b * 256 : (b + 1) * 256, :])
                scores.append(jnp.where(column <= row, s, masked_score) if b == r else s)
            peak = row_max(scores)
            total = 0
            for b in range(r + 1):
                total = total + jnp.dot(weights(scores[b], peak), own_v[b], preferred_element_type=F32)
            o_ref[:, h * 128 : (h + 1) * 128] = (total[:, :128] / total[:, 128:]).astype(BF16)
            found = jnp.where(lane == h, peak + jnp.log2(total[:, 128:]), found)
        lse_ref[...] = found

    @pl.when(pl.program_id(1) == 0)
    def _():
        half(0)

    @pl.when(pl.program_id(1) == 1)
    def _():
        half(1)


def anchor_kernel(lengths, q_ref, own_ref, lse_ref, near_ref, far_ref, *rest):
    o_ref = rest[-1]
    host = lax.axis_index("hst")
    _, x, _ = place()
    anchor_len = jnp.where(host > 0, lengths[0], 0)
    own_len = lengths[host] - pl.program_id(1) * 256
    valid = lax.broadcasted_iota(jnp.int32, (256, 128), 0) < own_len
    column = lax.broadcasted_iota(jnp.int32, (1, 256), 1)
    values = ones_beside(jnp.concatenate([near_ref[256:512, :], far_ref[256:512, :]], axis=0))
    near_ok, far_ok = column + x * 256 < anchor_len, column + (1 - x) * 256 < anchor_len
    for h in range(8):
        at = slice(h * 128, (h + 1) * 128)
        q = q_ref[:, at]
        near = jnp.where(near_ok, dot_t(q, near_ref[0:256, :]), masked_score)
        far = jnp.where(far_ok, dot_t(q, far_ref[0:256, :]), masked_score)
        lse = jnp.broadcast_to(lse_ref[:, h : h + 1], (256, 128))
        peak = jnp.maximum(row_max([near, far]), lse)
        w = jnp.concatenate([weights(near, peak), weights(far, peak)], axis=1)
        total = jnp.dot(w, values, preferred_element_type=F32)
        own = jnp.exp2(lse - peak)
        result = (total[:, :128] + own * own_ref[:, at].astype(F32)) / (total[:, 128:] + own)
        o_ref[:, at] = jnp.where(valid, result, 0.0).astype(BF16)


def body(ctx_query, ctx_key, context_value, lengths, owner, ask_query, ask_key, candidate_value_rows, out_weight):
    z, x, c = place()
    ask = [ask_query, ask_key, candidate_value_rows]
    dma = pltpu.SemaphoreType.DMA

    def send(array, pairs):
        return lax.ppermute(array, "hst", pairs)

    def after(array, *others):
        return lax.optimization_barrier((array, *others))[0]

    own_out, lse = None, []

    def own(g, *others):
        nonlocal own_out
        block = pl.BlockSpec((256, 1024), lambda j, i, g=g: (i, 2 * g + j))
        head = pl.BlockSpec((512, 128), lambda j, i, g=g: (0, 2 * g + j))
        own_out, found = call(
            own_kernel, [pltpu.HBM((512, 4096), BF16), pltpu.HBM((1024, 128), F32)],
            [block, head, head] + ([] if g == 0 else [ANY]),
            [block, pl.BlockSpec((256, 128), lambda j, i: (2 * j + i, 0))],
            in_hbm(ctx_query, ctx_key, context_value) + ([] if g == 0 else in_hbm(own_out)),
            after=others, grid=(2, 2), aliases={} if g == 0 else {3: 0}, flops=8 * 4096 * 768 * 256, data=2**22, vmem=16,
        )
        lse.append(found)
        return found

    ctx_out = None

    def encode(g, n, *others):
        nonlocal ctx_out
        block = pl.BlockSpec((256, 1024), lambda j, i, _, g=g: (i, g + j))
        half = pl.BlockSpec((512, 128), lambda j, i, _, g=g: (0, g + j))
        logs = pl.BlockSpec((256, 128), lambda j, i, _, g=g: ((g % 2 + j) * 2 + i, 0))
        ctx_out = call(
            anchor_kernel, pltpu.HBM((512, 4096), BF16),
            [block, block, logs, half, half] + ([] if g == 0 else [ANY]),
            block,
            in_hbm(ctx_query, own_out, lse[g // 2]) + halves + ([] if g == 0 else in_hbm(ctx_out)),
            scalars=[lengths], after=others, grid=(n, 2), aliases={} if g == 0 else {5: 0},
            flops=n * 4 * 4096 * 512 * 256, data=2**21, vmem=16,
        )
        return ctx_out

    kv = call(
        kv_pack_kernel,
        [pltpu.HBM((1024, 128), BF16)] + [shape((1024, 128), BF16)] * 3 + [pltpu.HBM((512, 512), BF16)] * 2,
        [ANY] * 2, [WHOLE] * 6, in_hbm(ctx_key, context_value), scratch=[dma((12,))],
    )
    packed = call(
        ask_pack_kernel, shape((128, 5120), BF16), [ANY] * 3, WHOLE, in_hbm(*ask), after=[kv[0]], scratch=[dma((6,))]
    )
    got_c = in_hbm(swap(packed, 1))
    kv_z = [kv[0]] + [swap(kv[s], 4 * s) for s in (1, 2, 3)]
    got = send(after(kv[5], packed), [(0, 2)])
    sent = call(
        x_pack_kernel, shape((64, 6144), BF16), [ANY] * 4, WHOLE, got_c + in_hbm(*ask), scalars=[owner],
        scratch=[dma((5,))],
    )
    got_x = swap(sent, 2)

    tick = own(0, sent)
    near = jnp.where(x == 0, kv[4], after(got, tick))
    got = send(near, [(i, i + 8) for i in (0, 2)])
    first = jnp.concatenate([kv[0], after(kv_z[1], tick)], axis=0)
    first_x = swap(first, 2)
    tick = own(1, near, kv_z[1])
    parts = call(
        z_pack_kernel, [pltpu.HBM((64, 1536), BF16)] + [shape((64, 1536), BF16)] * 3, [ANY, WHOLE] + [ANY] * 3,
        [WHOLE] * 4, got_c + in_vmem(got_x) + in_hbm(*ask), scalars=[owner], after=[tick], scratch=[dma((20,))],
    )
    asked = [parts[0]] + [swap(parts[s], 4 * s) for s in (1, 2, 3)]
    near = jnp.where(z == 0, near, after(got, parts[0]))
    got = send(near, [(i, i + 4) for i in (0, 2, 8, 10)])
    second = jnp.concatenate([after(kv_z[2], parts[0]), kv_z[3]], axis=0)
    second_x = swap(second, 2)

    level = z ^ (owner[0] // 4)
    own_kv = asked[0][:, 1024:]
    for s in (1, 2, 3):
        own_kv = jnp.where(level == s, asked[s][:, 1024:], own_kv)
    other_kv = swap(own_kv, 1)
    pairs = [first, second, first_x, second_x]
    pairs += [swap(after(part, own_kv), 1) for part in pairs]
    near = jnp.where(z % 2 == 0, near, after(got, own_kv))
    far = swap(near, 2)
    near_c = send(near, [(i, i + 1) for i in range(0, 16, 2)])
    answer = call(
        read_kernel, shape((64, 1024), BF16), [WHOLE] * 14, pl.BlockSpec((64, 512), lambda i, *_: (0, i)),
        [asked[0]] + in_vmem(*asked[1:], own_kv, other_kv, *pairs),
        scalars=[owner, lengths], grid=(2,),
        scratch=[pltpu.VMEM((256, 128), BF16)], flops=4 * 512 * 8192 * 256, data=2**22, vmem=20,
    )

    far = after(far, answer)
    halves = [jnp.where(c == 0, near, after(near_c, answer))]
    halves.append(jnp.where(c == 0, far, send(far, [(i, i + 1) for i in range(0, 16, 2)])))

    across = [swap(answer, 4 * s) for s in (1, 2, 3)]
    side = swap(answer, 2)
    tick = encode(0, 2, answer)
    across = [after(part, tick) for part in across]
    sides = [swap(part, 2) for part in across]
    near = jnp.stack([answer] + across + [after(side, tick)])
    near_far = swap(near, 1)
    tick = encode(2, 1)
    side = jnp.stack([after(part, tick) for part in sides])
    side_far = swap(side, 1)
    keep, sent = call(
        project_kernel, [shape((128, 512), F32), shape((128, 512), BF16)], [WHOLE] * 5, [WHOLE] * 2,
        in_vmem(near, near_far, side, side_far, out_weight), scratch=[pltpu.VMEM((256, 512), F32)],
        flops=2 * 256 * 4096 * 512, data=2**22, vmem=16,
    )
    got = lax.ppermute(sent, "tensor", [(0, 1), (1, 0)])
    tick = encode(3, 1, sent)
    return ctx_out, (keep + after(got, tick).astype(F32)).astype(BF16)


def solution(mesh):
    placed = (
        P("hst", "tensor"),
        P("hst", "tensor"),
        P("hst", "tensor"),
        P(),
        P(),
        P("hst", None, "tensor"),
        P("hst", None, "tensor"),
        P("hst", None, "tensor"),
        P("tensor", "hst"),
    )
    fits = dict(mesh.shape) == {"hst": 16, "tensor": 2}
    return jax.shard_map(
        body if fits else generic_body,
        mesh=mesh,
        in_specs=placed,
        out_specs=(P("hst", "tensor"), P("tensor", "hst")),
        check_vma=False,
    )
```

```python
import functools
import math

import jax
import jax.numpy as jnp
from jax import lax
from jax.experimental import pallas as pl
from jax.experimental.pallas import tpu as pltpu
from jax.sharding import PartitionSpec as P

HEAD_SIZE = 128
F32 = jnp.float32
BF16 = jnp.bfloat16
LOG_SCALE = math.log2(math.e) / math.sqrt(HEAD_SIZE)


masked_score = -1e30


def broadcast(block, axis, owner):
    block = jnp.where(lax.axis_index(axis) == owner, block, jnp.zeros_like(block))
    return lax.psum(block, axis)


def combined_all(array, axis, combine):
    everything = jax.tree.map(lambda part: lax.all_gather(part, axis), array)
    first = jax.tree.map(lambda part: part[0], everything)

    def hop(k, so_far):
        return combine(so_far, jax.tree.map(lambda part: part[k], everything))

    return lax.fori_loop(1, lax.axis_size(axis), hop, first)


def partial_attend(queries, keys, values, allowed):
    rows = queries.shape[0]
    groups = keys.shape[1] // HEAD_SIZE
    query_heads = queries.reshape(rows, groups, -1, HEAD_SIZE)
    key_heads = keys.reshape(keys.shape[0], groups, HEAD_SIZE)
    value_heads = values.reshape(values.shape[0], groups, HEAD_SIZE)
    scores = jnp.einsum(
        "rkgd,skd->rkgs", query_heads, key_heads, preferred_element_type=jnp.float32
    ) / math.sqrt(HEAD_SIZE)
    scores = jnp.where(allowed[:, None, None, :], scores, masked_score)
    peaks = jnp.max(scores, axis=-1)
    weights = jnp.exp(scores - peaks[..., None]).astype(jnp.bfloat16)
    totals = jnp.sum(weights.astype(jnp.float32), axis=-1)
    outputs = jnp.einsum("rkgs,skd->rkgd", weights, value_heads, preferred_element_type=jnp.float32)
    return (peaks.reshape(rows, -1), totals.reshape(rows, -1), outputs.reshape(rows, -1))


def normalize(outputs, totals):
    rows, heads = totals.shape
    return (outputs.reshape(rows, heads, -1) / totals[..., None]).reshape(rows, -1)


def combine(first_piece, second_piece):
    rows, heads = first_piece[0].shape
    top = jnp.maximum(first_piece[0], second_piece[0])
    scale_one = jnp.exp(first_piece[0] - top)
    scale_two = jnp.exp(second_piece[0] - top)
    totals = scale_one * first_piece[1] + scale_two * second_piece[1]
    outputs = (
        first_piece[2].reshape(rows, heads, -1) * scale_one[..., None]
        + second_piece[2].reshape(rows, heads, -1) * scale_two[..., None]
    )
    return (top, totals, outputs.reshape(rows, -1))


def generic_body(
    ctx_query,
    ctx_key,
    context_value,
    lengths,
    owner,
    ask_query,
    ask_key,
    candidate_value_rows,
    out_weight,
):
    host = lax.axis_index("hst")
    anchor_key, anchor_value = (broadcast(ctx_key, "hst", 0), broadcast(context_value, "hst", 0))
    block_len = ctx_query.shape[0]
    own_len = lengths[host]
    anchor_len = lengths[0]
    keys_all = jnp.concatenate([anchor_key, ctx_key], axis=0)
    values_all = jnp.concatenate([anchor_value, context_value], axis=0)
    rows_each = min(512, block_len)
    columns = jnp.arange(block_len, dtype=jnp.int32)
    row_pos = 0 + jnp.arange(rows_each, dtype=jnp.int32)
    anchor_ok = jnp.broadcast_to(
        (columns[None, :] < anchor_len) & (host > 0), (rows_each, block_len)
    )
    own_ok = (columns[None, :] <= row_pos[:, None]) & (columns[None, :] < own_len)
    allowed = jnp.concatenate([anchor_ok, own_ok], axis=1)
    peaks, totals, outputs = partial_attend(ctx_query, keys_all, values_all, allowed)
    result = jnp.where(row_pos[:, None] < own_len, normalize(outputs, totals), 0.0)
    pieces = result.astype(jnp.bfloat16)
    chosen = owner[0]
    query_rows = ask_query.shape[1]
    query_pos = jnp.arange(query_rows, dtype=jnp.int32)
    causal = query_pos[None, :] <= query_pos[:, None]
    block_ok = jnp.broadcast_to((columns < own_len)[None, :], (query_rows, block_len))
    asked, ask_keys, ask_values = (
        broadcast(ask_query[0], "hst", chosen),
        broadcast(ask_key[0], "hst", chosen),
        broadcast(candidate_value_rows[0], "hst", chosen),
    )
    local = partial_attend(asked, ctx_key, context_value, block_ok)
    pending = partial_attend(asked, ask_keys, ask_values, causal)
    merged = combined_all(local, "hst", combine)
    merged = combine(merged, pending)
    answer = normalize(merged[2], merged[1]).astype(jnp.bfloat16)
    projected = jnp.dot(answer, out_weight, preferred_element_type=jnp.float32)
    layer_out = lax.psum_scatter(
        projected.astype(jnp.bfloat16), "tensor", scatter_dimension=0, tiled=True
    )
    return (pieces, layer_out)


def dot_t(a, b):
    return lax.dot_general(a, b, (((1,), (1,)), ((), ())), preferred_element_type=F32)


def swap(array, bit):
    return lax.ppermute(array, "hst", [(i, i ^ bit) for i in range(16)])


def place():
    host = lax.axis_index("hst")
    return host // 4, host // 2 % 2, host % 2


def call(
    kernel, out_shape, in_specs, out_specs, args, scalars=(), after=(), grid=(), scratch=(), flops=0, data=0, aliases=None, vmem=8
):
    n, m = len(scalars), len(after)

    def body(*refs):
        kernel(*refs[:n], *refs[n + m :])

    return pl.pallas_call(
        body,
        grid_spec=pltpu.PrefetchScalarGridSpec(
            num_scalar_prefetch=n,
            grid=grid,
            in_specs=[pl.BlockSpec(memory_space=pl.ANY)] * m + in_specs,
            out_specs=out_specs,
            scratch_shapes=list(scratch),
        ),
        out_shape=out_shape,
        input_output_aliases={n + m + i: o for i, o in (aliases or {}).items()},
        compiler_params=pltpu.CompilerParams(vmem_limit_bytes=vmem * 2**20),
        cost_estimate=pl.CostEstimate(flops=flops, bytes_accessed=data, transcendentals=0),
    )(*scalars, *after, *args)


shape = jax.ShapeDtypeStruct
WHOLE = pl.BlockSpec(memory_space=pltpu.VMEM)
ANY = pl.BlockSpec(memory_space=pl.ANY)


def in_hbm(*arrays):
    return [pltpu.with_memory_space_constraint(array, pltpu.HBM) for array in arrays]


def in_vmem(*arrays):
    return [pltpu.with_memory_space_constraint(array, pltpu.VMEM) for array in arrays]


def lanes(start, size):
    return pl.ds(pl.multiple_of(start, 128), size)


def rows(start, size):
    return pl.ds(pl.multiple_of(start, 64), size)


def copy_all(pairs, sems):
    copies = [pltpu.make_async_copy(a, b, sems.at[i]) for i, (a, b) in enumerate(pairs)]
    for copy in copies:
        copy.start()
    for copy in copies:
        copy.wait()


def ask_pack_kernel(q_ref, k_ref, v_ref, out_ref, sems):
    _, _, c = place()
    pairs = []
    for x in range(2):
        here, there = rows(x * 128 + (1 - c) * 64, 64), slice(x * 64, (x + 1) * 64)
        pairs += [
            (q_ref.at[0, here], out_ref.at[there, 0:4096]),
            (k_ref.at[0, here], out_ref.at[there, 4096:4608]),
            (v_ref.at[0, here], out_ref.at[there, 4608:5120]),
        ]
    copy_all(pairs, sems)


def kv_pack_kernel(k_ref, v_ref, *refs):
    z, _, _ = place()
    sems, pairs = refs[6], []
    for s, out_ref in enumerate(refs[:4]):
        head = lanes((z ^ s) * 128, 128)
        pairs += [(k_ref.at[:, head], out_ref.at[0:512]), (v_ref.at[:, head], out_ref.at[512:1024])]
    for i, out_ref in enumerate(refs[4:6]):
        here = slice(i * 256, (i + 1) * 256)
        pairs += [(k_ref.at[here], out_ref.at[0:256]), (v_ref.at[here], out_ref.at[256:512])]
    copy_all(pairs, sems)


def x_pack_kernel(owner, got_ref, q_ref, k_ref, v_ref, send_ref, sems):
    _, x, c = place()
    owner_c = owner[0] % 2

    @pl.when(owner_c == c)
    def _():
        pairs = [(q_ref.at[0, rows((1 - x) * 128 + c * 64, 64)], send_ref.at[:, 0:4096])]
        for i in range(2):
            here, to = rows(i * 128 + c * 64, 64), 4096 + i * 1024
            pairs += [
                (k_ref.at[0, here], send_ref.at[:, to : to + 512]),
                (v_ref.at[0, here], send_ref.at[:, to + 512 : to + 1024]),
            ]
        copy_all(pairs, sems)

    @pl.when(owner_c != c)
    def _():
        pairs = [(got_ref.at[rows((1 - x) * 64, 64), 0:4096], send_ref.at[:, 0:4096])]
        for i in range(2):
            to = 4096 + i * 1024
            pairs += [(got_ref.at[i * 64 : (i + 1) * 64, 4096:5120], send_ref.at[:, to : to + 1024])]
        copy_all(pairs, sems)


def z_pack_kernel(owner, c_ref, x_ref, q_ref, k_ref, v_ref, *refs):
    z, x, c = place()
    outs, sems = refs[:4], refs[4]
    owner_c, owner_x = owner[0] % 2, owner[0] // 2 % 2

    @pl.when(owner_x != x)
    def _():
        for s, out_ref in enumerate(outs):
            j = z ^ s
            out_ref[:, 0:1024] = x_ref[:, lanes(j * 1024, 1024)]
            for i in range(4):
                out_ref[:, 1024 + i * 128 : 1152 + i * 128] = x_ref[:, lanes(4096 + i * 512 + j * 128, 128)]

    @pl.when((owner_x == x) & (owner_c == c))
    def _():
        pairs = []
        for s, out_ref in enumerate(outs):
            j = z ^ s
            pairs.append((q_ref.at[0, rows(x * 128 + c * 64, 64), lanes(j * 1024, 1024)], out_ref.at[:, 0:1024]))
            for i in range(4):
                part = (k_ref, v_ref)[i % 2].at[0, rows(i // 2 * 128 + c * 64, 64), lanes(j * 128, 128)]
                pairs.append((part, out_ref.at[:, 1024 + i * 128 : 1152 + i * 128]))
        copy_all(pairs, sems)

    @pl.when((owner_x == x) & (owner_c != c))
    def _():
        pairs = []
        for s, out_ref in enumerate(outs):
            j = z ^ s
            pairs.append((c_ref.at[rows(x * 64, 64), lanes(j * 1024, 1024)], out_ref.at[:, 0:1024]))
            for i in range(4):
                part = c_ref.at[i // 2 * 64 : (i // 2 + 1) * 64, lanes(4096 + i % 2 * 512 + j * 128, 128)]
                pairs.append((part, out_ref.at[:, 1024 + i * 128 : 1152 + i * 128]))
        copy_all(pairs, sems)


def ones_beside(values):
    return jnp.concatenate([values, jnp.ones(values.shape, values.dtype)], axis=1)


def read_kernel(owner, lengths, *refs):
    asked, (own_kv, other_kv), pairs, (out_ref, q_ref) = refs[:4], refs[4:6], refs[6:14], refs[14:]
    z, x, c = place()
    step = pl.program_id(0)
    at = z ^ (owner[0] // 4)
    for s in range(4):

        @pl.when(at == s)
        def _(s=s):
            for h in range(4):
                q_ref[h * 64 : (h + 1) * 64, :] = asked[s][:, lanes(step * 512 + h * 128, 128)]

    q = q_ref[...]
    column = lax.broadcasted_iota(jnp.int32, (1, 512), 1)
    found = []

    def add(scores, values):
        peak = row_max(scores)
        total = 0
        for s, v in zip(scores, values):
            total = total + jnp.dot(weights(s, peak), ones_beside(v), preferred_element_type=F32)
        found.append((peak, total))

    for pair, ref in enumerate(pairs):
        scores, values = [], []
        for i in range(2):
            block = ((z ^ (pair % 2 * 2 + i)) * 2 + (x ^ (pair // 2 % 2))) * 2 + (c ^ (pair // 4))
            k, v = ref[i * 1024 : i * 1024 + 512, :], ref[i * 1024 + 512 : (i + 1) * 1024, :]
            scores.append(jnp.where(column < lengths[block], dot_t(q, k), masked_score))
            values.append(v)
        add(scores, values)
    row_at = lax.broadcasted_iota(jnp.int32, (256, 64), 0) % 64 + x * 128 + c * 64
    column = lax.broadcasted_iota(jnp.int32, (256, 64), 1)
    scores, values = [], []
    for ref, core in ((own_kv, c), (other_kv, 1 - c)):
        for i in range(2):
            s = dot_t(q, ref[:, i * 256 : i * 256 + 128])
            scores.append(jnp.where(column + i * 128 + core * 64 <= row_at, s, masked_score))
            values.append(ref[:, i * 256 + 128 : (i + 1) * 256])
    add([jnp.concatenate(scores, axis=1)], [jnp.concatenate(values, axis=0)])
    top = functools.reduce(jnp.maximum, [peak for peak, _ in found])
    scales = [jnp.exp2(peak - top) for peak, _ in found]
    sums = sum(scale * part[:, :128] for scale, (_, part) in zip(scales, found))
    total = sum(scale * part[:, 128:] for scale, (_, part) in zip(scales, found))
    answer = (sums / total).astype(BF16)
    for h in range(4):
        out_ref[:, h * 128 : (h + 1) * 128] = answer[h * 64 : (h + 1) * 64, :]


def project_kernel(*refs):
    near, near_far, side, side_far, w_ref, keep_ref, send_ref, sum_ref = refs
    z, x, c = place()
    t = lax.axis_index("tensor")
    for s in range(4):
        w = w_ref[pl.ds(pl.multiple_of((z ^ s) * 1024, 1024), 1024), :]
        across = [(near, s), (near_far, s), (near, 4) if s == 0 else (side, s - 1), (near_far, 4) if s == 0 else (side_far, s - 1)]
        a = jnp.concatenate([ref[i] for ref, i in across], axis=0)
        product = jnp.dot(a, w, preferred_element_type=F32)
        if s == 0:
            sum_ref[...] = product
        else:
            sum_ref[...] += product
    for r in range(4):
        half, core = x ^ (r // 2), c ^ (r % 2)
        at_row = rows(core * 64, 64)
        quarter = sum_ref[r * 64 : (r + 1) * 64, :]

        @pl.when(half == t)
        def _(quarter=quarter, at_row=at_row):
            keep_ref[at_row, :] = quarter

        @pl.when(half != t)
        def _(quarter=quarter, at_row=at_row):
            send_ref[at_row, :] = quarter.astype(BF16)


def row_max(scores):
    tiles = [s[:, i : i + 128] for s in scores for i in range(0, s.shape[1], 128)]
    peak = jnp.max(functools.reduce(jnp.maximum, tiles), axis=1, keepdims=True)
    return jnp.broadcast_to(peak * LOG_SCALE, (scores[0].shape[0], 128))


def weights(s, peak):
    tiles = [jnp.exp2(s[:, i : i + 128] * LOG_SCALE - peak).astype(BF16) for i in range(0, s.shape[1], 128)]
    return jnp.concatenate(tiles, axis=1)


def own_kernel(q_ref, k_ref, v_ref, *rest):
    o_ref, lse_ref = rest[-2:]
    row = lax.broadcasted_iota(jnp.int32, (256, 256), 0)
    column = lax.broadcasted_iota(jnp.int32, (256, 256), 1)
    lane = lax.broadcasted_iota(jnp.int32, (256, 128), 1)

    def half(r):
        own_v = [ones_beside(v_ref[b * 256 : (b + 1) * 256, :]) for b in range(r + 1)]
        found = jnp.zeros((256, 128), F32)
        for h in range(8):
            q = q_ref[:, h * 128 : (h + 1) * 128]
            scores = []
            for b in range(r + 1):
                s = dot_t(q, k_ref[b * 256 : (b + 1) * 256, :])
                scores.append(jnp.where(column <= row, s, masked_score) if b == r else s)
            peak = row_max(scores)
            total = 0
            for b in range(r + 1):
                total = total + jnp.dot(weights(scores[b], peak), own_v[b], preferred_element_type=F32)
            o_ref[:, h * 128 : (h + 1) * 128] = (total[:, :128] / total[:, 128:]).astype(BF16)
            found = jnp.where(lane == h, peak + jnp.log2(total[:, 128:]), found)
        lse_ref[...] = found

    @pl.when(pl.program_id(1) == 0)
    def _():
        half(0)

    @pl.when(pl.program_id(1) == 1)
    def _():
        half(1)


def anchor_kernel(lengths, q_ref, own_ref, lse_ref, near_ref, far_ref, near_c_ref, far_c_ref, *rest):
    o_ref = rest[-1]
    host = lax.axis_index("hst")
    _, x, c = place()
    near_half = jnp.where(c == 0, near_ref[...], near_c_ref[...])
    far_half = jnp.where(c == 0, far_ref[...], far_c_ref[...])
    anchor_len = jnp.where(host > 0, lengths[0], 0)
    own_len = lengths[host] - pl.program_id(1) * 256
    valid = lax.broadcasted_iota(jnp.int32, (256, 128), 0) < own_len
    column = lax.broadcasted_iota(jnp.int32, (1, 256), 1)
    values = ones_beside(jnp.concatenate([near_half[256:512, :], far_half[256:512, :]], axis=0))
    near_ok, far_ok = column + x * 256 < anchor_len, column + (1 - x) * 256 < anchor_len
    for h in range(8):
        at = slice(h * 128, (h + 1) * 128)
        q = q_ref[:, at]
        near = jnp.where(near_ok, dot_t(q, near_half[0:256, :]), masked_score)
        far = jnp.where(far_ok, dot_t(q, far_half[0:256, :]), masked_score)
        lse = jnp.broadcast_to(lse_ref[:, h : h + 1], (256, 128))
        peak = jnp.maximum(row_max([near, far]), lse)
        w = jnp.concatenate([weights(near, peak), weights(far, peak)], axis=1)
        total = jnp.dot(w, values, preferred_element_type=F32)
        own = jnp.exp2(lse - peak)
        result = (total[:, :128] + own * own_ref[:, at].astype(F32)) / (total[:, 128:] + own)
        o_ref[:, at] = jnp.where(valid, result, 0.0).astype(BF16)


def body(ctx_query, ctx_key, context_value, lengths, owner, ask_query, ask_key, candidate_value_rows, out_weight):
    z, x, c = place()
    ask = [ask_query, ask_key, candidate_value_rows]
    dma = pltpu.SemaphoreType.DMA

    def send(array, pairs):
        return lax.ppermute(array, "hst", pairs)

    def after(array, *others):
        return lax.optimization_barrier((array, *others))[0]

    own_out, lse = None, []

    def own(g, *others):
        nonlocal own_out
        block = pl.BlockSpec((256, 1024), lambda j, i, g=g: (i, 2 * g + j))
        head = pl.BlockSpec((512, 128), lambda j, i, g=g: (0, 2 * g + j))
        own_out, found = call(
            own_kernel, [pltpu.HBM((512, 4096), BF16), pltpu.HBM((1024, 128), F32)],
            [block, head, head] + ([] if g == 0 else [ANY]),
            [block, pl.BlockSpec((256, 128), lambda j, i: (2 * j + i, 0))],
            in_hbm(ctx_query, ctx_key, context_value) + ([] if g == 0 else in_hbm(own_out)),
            after=others, grid=(2, 2), aliases={} if g == 0 else {3: 0}, flops=8 * 4096 * 768 * 256, data=2**22, vmem=16,
        )
        lse.append(found)
        return found

    ctx_out = None

    def encode(g, n, *others):
        nonlocal ctx_out
        block = pl.BlockSpec((256, 1024), lambda j, i, _, g=g: (i, g + j))
        half = pl.BlockSpec((512, 128), lambda j, i, _, g=g: (0, g + j))
        logs = pl.BlockSpec((256, 128), lambda j, i, _, g=g: ((g % 2 + j) * 2 + i, 0))
        ctx_out = call(
            anchor_kernel, pltpu.HBM((512, 4096), BF16),
            [block, block, logs] + [half] * 4 + ([] if g == 0 else [ANY]),
            block,
            in_hbm(ctx_query, own_out, lse[g // 2]) + halves + ([] if g == 0 else in_hbm(ctx_out)),
            scalars=[lengths], after=others, grid=(n, 2), aliases={} if g == 0 else {7: 0},
            flops=n * 4 * 4096 * 512 * 256, data=2**21, vmem=16,
        )
        return ctx_out

    packed = call(
        ask_pack_kernel, shape((128, 5120), BF16), [ANY] * 3, WHOLE, in_hbm(*ask), scratch=[dma((6,))]
    )
    kv = call(
        kv_pack_kernel,
        [pltpu.HBM((1024, 128), BF16)] + [shape((1024, 128), BF16)] * 3 + [pltpu.HBM((512, 512), BF16)] * 2,
        [ANY] * 2, [WHOLE] * 6, in_hbm(ctx_key, context_value), after=[packed], scratch=[dma((12,))],
    )
    got_c = in_hbm(swap(packed, 1))
    kv_z = [kv[0]] + [swap(kv[s], 4 * s) for s in (1, 2, 3)]
    got = send(after(kv[5], packed), [(0, 2)])
    sent = call(
        x_pack_kernel, shape((64, 6144), BF16), [ANY] * 4, WHOLE, got_c + in_hbm(*ask), scalars=[owner],
        scratch=[dma((5,))],
    )
    got_x = swap(sent, 2)

    tick = own(0, sent)
    near = jnp.where(x == 0, kv[4], after(got, tick))
    got = send(near, [(i, i + 8) for i in (0, 2)])
    first = jnp.concatenate([kv[0], after(kv_z[1], tick)], axis=0)
    first_x = swap(first, 2)
    tick = own(1, near, kv_z[1])
    parts = call(
        z_pack_kernel, [pltpu.HBM((64, 1536), BF16)] + [shape((64, 1536), BF16)] * 3, [ANY, WHOLE] + [ANY] * 3,
        [WHOLE] * 4, got_c + in_vmem(got_x) + in_hbm(*ask), scalars=[owner], after=[tick], scratch=[dma((20,))],
    )
    asked = [parts[0]] + [swap(parts[s], 4 * s) for s in (1, 2, 3)]
    near = jnp.where(z == 0, near, after(got, parts[0]))
    got = send(near, [(i, i + 4) for i in (0, 2, 8, 10)])
    second = jnp.concatenate([after(kv_z[2], parts[0]), kv_z[3]], axis=0)
    second_x = swap(second, 2)

    level = z ^ (owner[0] // 4)
    own_kv = asked[0][:, 1024:]
    for s in (1, 2, 3):
        own_kv = jnp.where(level == s, asked[s][:, 1024:], own_kv)
    other_kv = swap(own_kv, 1)
    pairs = [first, second, first_x, second_x]
    pairs += [swap(after(part, own_kv), 1) for part in pairs]
    near = jnp.where(z % 2 == 0, near, after(got, own_kv))
    far = swap(near, 2)
    near_c = send(near, [(i, i + 1) for i in range(0, 16, 2)])
    answer = call(
        read_kernel, shape((64, 1024), BF16), [WHOLE] * 14, pl.BlockSpec((64, 512), lambda i, *_: (0, i)),
        [asked[0]] + in_vmem(*asked[1:], own_kv, other_kv, *pairs),
        scalars=[owner, lengths], grid=(2,),
        scratch=[pltpu.VMEM((256, 128), BF16)], flops=4 * 512 * 8192 * 256, data=2**22, vmem=20,
    )

    far = after(far, answer)
    halves = [near, far, after(near_c, answer), send(far, [(i, i + 1) for i in range(0, 16, 2)])]

    across = [swap(answer, 4 * s) for s in (1, 2, 3)]
    side = swap(answer, 2)
    tick = encode(0, 2, answer)
    across = [after(part, tick) for part in across]
    sides = [swap(part, 2) for part in across]
    near = jnp.stack([answer] + across + [after(side, tick)])
    near_far = swap(near, 1)
    tick = encode(2, 1)
    side = jnp.stack([after(part, tick) for part in sides])
    side_far = swap(side, 1)
    keep, sent = call(
        project_kernel, [shape((128, 512), F32), shape((128, 512), BF16)], [WHOLE] * 5, [WHOLE] * 2,
        in_vmem(near, near_far, side, side_far, out_weight), scratch=[pltpu.VMEM((256, 512), F32)],
        flops=2 * 256 * 4096 * 512, data=2**22, vmem=16,
    )
    got = lax.ppermute(sent, "tensor", [(0, 1), (1, 0)])
    tick = encode(3, 1, sent)
    return ctx_out, (keep + after(got, tick).astype(F32)).astype(BF16)


def solution(mesh):
    placed = (
        P("hst", "tensor"),
        P("hst", "tensor"),
        P("hst", "tensor"),
        P(),
        P(),
        P("hst", None, "tensor"),
        P("hst", None, "tensor"),
        P("hst", None, "tensor"),
        P("tensor", "hst"),
    )
    fits = dict(mesh.shape) == {"hst": 16, "tensor": 2}
    return jax.shard_map(
        body if fits else generic_body,
        mesh=mesh,
        in_specs=placed,
        out_specs=(P("hst", "tensor"), P("tensor", "hst")),
        check_vma=False,
    )
```

```python
import functools
import math

import jax
import jax.numpy as jnp
from jax import lax
from jax.experimental import pallas as pl
from jax.experimental.pallas import tpu as pltpu
from jax.sharding import PartitionSpec as P

HEAD_SIZE = 128
F32 = jnp.float32
BF16 = jnp.bfloat16
LOG_SCALE = math.log2(math.e) / math.sqrt(HEAD_SIZE)


masked_score = -1e30


def broadcast(block, axis, owner):
    block = jnp.where(lax.axis_index(axis) == owner, block, jnp.zeros_like(block))
    return lax.psum(block, axis)


def combined_all(array, axis, combine):
    everything = jax.tree.map(lambda part: lax.all_gather(part, axis), array)
    first = jax.tree.map(lambda part: part[0], everything)

    def hop(k, so_far):
        return combine(so_far, jax.tree.map(lambda part: part[k], everything))

    return lax.fori_loop(1, lax.axis_size(axis), hop, first)


def partial_attend(queries, keys, values, allowed):
    rows = queries.shape[0]
    groups = keys.shape[1] // HEAD_SIZE
    query_heads = queries.reshape(rows, groups, -1, HEAD_SIZE)
    key_heads = keys.reshape(keys.shape[0], groups, HEAD_SIZE)
    value_heads = values.reshape(values.shape[0], groups, HEAD_SIZE)
    scores = jnp.einsum(
        "rkgd,skd->rkgs", query_heads, key_heads, preferred_element_type=jnp.float32
    ) / math.sqrt(HEAD_SIZE)
    scores = jnp.where(allowed[:, None, None, :], scores, masked_score)
    peaks = jnp.max(scores, axis=-1)
    weights = jnp.exp(scores - peaks[..., None]).astype(jnp.bfloat16)
    totals = jnp.sum(weights.astype(jnp.float32), axis=-1)
    outputs = jnp.einsum("rkgs,skd->rkgd", weights, value_heads, preferred_element_type=jnp.float32)
    return (peaks.reshape(rows, -1), totals.reshape(rows, -1), outputs.reshape(rows, -1))


def normalize(outputs, totals):
    rows, heads = totals.shape
    return (outputs.reshape(rows, heads, -1) / totals[..., None]).reshape(rows, -1)


def combine(first_piece, second_piece):
    rows, heads = first_piece[0].shape
    top = jnp.maximum(first_piece[0], second_piece[0])
    scale_one = jnp.exp(first_piece[0] - top)
    scale_two = jnp.exp(second_piece[0] - top)
    totals = scale_one * first_piece[1] + scale_two * second_piece[1]
    outputs = (
        first_piece[2].reshape(rows, heads, -1) * scale_one[..., None]
        + second_piece[2].reshape(rows, heads, -1) * scale_two[..., None]
    )
    return (top, totals, outputs.reshape(rows, -1))


def generic_body(
    ctx_query,
    ctx_key,
    context_value,
    lengths,
    owner,
    ask_query,
    ask_key,
    candidate_value_rows,
    out_weight,
):
    host = lax.axis_index("hst")
    anchor_key, anchor_value = (broadcast(ctx_key, "hst", 0), broadcast(context_value, "hst", 0))
    block_len = ctx_query.shape[0]
    own_len = lengths[host]
    anchor_len = lengths[0]
    keys_all = jnp.concatenate([anchor_key, ctx_key], axis=0)
    values_all = jnp.concatenate([anchor_value, context_value], axis=0)
    rows_each = min(512, block_len)
    columns = jnp.arange(block_len, dtype=jnp.int32)
    row_pos = 0 + jnp.arange(rows_each, dtype=jnp.int32)
    anchor_ok = jnp.broadcast_to(
        (columns[None, :] < anchor_len) & (host > 0), (rows_each, block_len)
    )
    own_ok = (columns[None, :] <= row_pos[:, None]) & (columns[None, :] < own_len)
    allowed = jnp.concatenate([anchor_ok, own_ok], axis=1)
    peaks, totals, outputs = partial_attend(ctx_query, keys_all, values_all, allowed)
    result = jnp.where(row_pos[:, None] < own_len, normalize(outputs, totals), 0.0)
    pieces = result.astype(jnp.bfloat16)
    chosen = owner[0]
    query_rows = ask_query.shape[1]
    query_pos = jnp.arange(query_rows, dtype=jnp.int32)
    causal = query_pos[None, :] <= query_pos[:, None]
    block_ok = jnp.broadcast_to((columns < own_len)[None, :], (query_rows, block_len))
    asked, ask_keys, ask_values = (
        broadcast(ask_query[0], "hst", chosen),
        broadcast(ask_key[0], "hst", chosen),
        broadcast(candidate_value_rows[0], "hst", chosen),
    )
    local = partial_attend(asked, ctx_key, context_value, block_ok)
    pending = partial_attend(asked, ask_keys, ask_values, causal)
    merged = combined_all(local, "hst", combine)
    merged = combine(merged, pending)
    answer = normalize(merged[2], merged[1]).astype(jnp.bfloat16)
    projected = jnp.dot(answer, out_weight, preferred_element_type=jnp.float32)
    layer_out = lax.psum_scatter(
        projected.astype(jnp.bfloat16), "tensor", scatter_dimension=0, tiled=True
    )
    return (pieces, layer_out)


def dot_t(a, b):
    return lax.dot_general(a, b, (((1,), (1,)), ((), ())), preferred_element_type=F32)


def swap(array, bit):
    return lax.ppermute(array, "hst", [(i, i ^ bit) for i in range(16)])


def place():
    host = lax.axis_index("hst")
    return host // 4, host // 2 % 2, host % 2


def call(
    kernel, out_shape, in_specs, out_specs, args, scalars=(), after=(), grid=(), scratch=(), flops=0, data=0, aliases=None, vmem=8
):
    n, m = len(scalars), len(after)

    def body(*refs):
        kernel(*refs[:n], *refs[n + m :])

    return pl.pallas_call(
        body,
        grid_spec=pltpu.PrefetchScalarGridSpec(
            num_scalar_prefetch=n,
            grid=grid,
            in_specs=[pl.BlockSpec(memory_space=pl.ANY)] * m + in_specs,
            out_specs=out_specs,
            scratch_shapes=list(scratch),
        ),
        out_shape=out_shape,
        input_output_aliases={n + m + i: o for i, o in (aliases or {}).items()},
        compiler_params=pltpu.CompilerParams(vmem_limit_bytes=vmem * 2**20),
        cost_estimate=pl.CostEstimate(flops=flops, bytes_accessed=data, transcendentals=0),
    )(*scalars, *after, *args)


shape = jax.ShapeDtypeStruct
WHOLE = pl.BlockSpec(memory_space=pltpu.VMEM)
ANY = pl.BlockSpec(memory_space=pl.ANY)


def in_hbm(*arrays):
    return [pltpu.with_memory_space_constraint(array, pltpu.HBM) for array in arrays]


def in_vmem(*arrays):
    return [pltpu.with_memory_space_constraint(array, pltpu.VMEM) for array in arrays]


def lanes(start, size):
    return pl.ds(pl.multiple_of(start, 128), size)


def rows(start, size):
    return pl.ds(pl.multiple_of(start, 64), size)


def copy_all(pairs, sems):
    copies = [pltpu.make_async_copy(a, b, sems.at[i]) for i, (a, b) in enumerate(pairs)]
    for copy in copies:
        copy.start()
    for copy in copies:
        copy.wait()


def ask_pack_kernel(q_ref, k_ref, v_ref, out_ref, sems):
    _, _, c = place()
    pairs = []
    for x in range(2):
        here, there = rows(x * 128 + (1 - c) * 64, 64), slice(x * 64, (x + 1) * 64)
        pairs += [
            (q_ref.at[0, here], out_ref.at[there, 0:4096]),
            (k_ref.at[0, here], out_ref.at[there, 4096:4608]),
            (v_ref.at[0, here], out_ref.at[there, 4608:5120]),
        ]
    copy_all(pairs, sems)


def kv_pack_kernel(k_ref, v_ref, *refs):
    z, _, _ = place()
    sems, pairs = refs[6], []
    for s, out_ref in enumerate(refs[:4]):
        head = lanes((z ^ s) * 128, 128)
        pairs += [(k_ref.at[:, head], out_ref.at[0:512]), (v_ref.at[:, head], out_ref.at[512:1024])]
    for i, out_ref in enumerate(refs[4:6]):
        here = slice(i * 256, (i + 1) * 256)
        pairs += [(k_ref.at[here], out_ref.at[0:256]), (v_ref.at[here], out_ref.at[256:512])]
    copy_all(pairs, sems)


def x_pack_kernel(owner, got_ref, q_ref, k_ref, v_ref, send_ref, sems):
    _, x, c = place()
    owner_c = owner[0] % 2

    @pl.when(owner_c == c)
    def _():
        pairs = [(q_ref.at[0, rows((1 - x) * 128 + c * 64, 64)], send_ref.at[:, 0:4096])]
        for i in range(2):
            here, to = rows(i * 128 + c * 64, 64), 4096 + i * 1024
            pairs += [
                (k_ref.at[0, here], send_ref.at[:, to : to + 512]),
                (v_ref.at[0, here], send_ref.at[:, to + 512 : to + 1024]),
            ]
        copy_all(pairs, sems)

    @pl.when(owner_c != c)
    def _():
        pairs = [(got_ref.at[rows((1 - x) * 64, 64), 0:4096], send_ref.at[:, 0:4096])]
        for i in range(2):
            to = 4096 + i * 1024
            pairs += [(got_ref.at[i * 64 : (i + 1) * 64, 4096:5120], send_ref.at[:, to : to + 1024])]
        copy_all(pairs, sems)


def z_pack_kernel(owner, c_ref, x_ref, q_ref, k_ref, v_ref, *refs):
    z, x, c = place()
    outs, sems = refs[:4], refs[4]
    owner_c, owner_x = owner[0] % 2, owner[0] // 2 % 2

    @pl.when(owner_x != x)
    def _():
        for s, out_ref in enumerate(outs):
            j = z ^ s
            out_ref[:, 0:1024] = x_ref[:, lanes(j * 1024, 1024)]
            for i in range(4):
                out_ref[:, 1024 + i * 128 : 1152 + i * 128] = x_ref[:, lanes(4096 + i * 512 + j * 128, 128)]

    @pl.when((owner_x == x) & (owner_c == c))
    def _():
        pairs = []
        for s, out_ref in enumerate(outs):
            j = z ^ s
            pairs.append((q_ref.at[0, rows(x * 128 + c * 64, 64), lanes(j * 1024, 1024)], out_ref.at[:, 0:1024]))
            for i in range(4):
                part = (k_ref, v_ref)[i % 2].at[0, rows(i // 2 * 128 + c * 64, 64), lanes(j * 128, 128)]
                pairs.append((part, out_ref.at[:, 1024 + i * 128 : 1152 + i * 128]))
        copy_all(pairs, sems)

    @pl.when((owner_x == x) & (owner_c != c))
    def _():
        pairs = []
        for s, out_ref in enumerate(outs):
            j = z ^ s
            pairs.append((c_ref.at[rows(x * 64, 64), lanes(j * 1024, 1024)], out_ref.at[:, 0:1024]))
            for i in range(4):
                part = c_ref.at[i // 2 * 64 : (i // 2 + 1) * 64, lanes(4096 + i % 2 * 512 + j * 128, 128)]
                pairs.append((part, out_ref.at[:, 1024 + i * 128 : 1152 + i * 128]))
        copy_all(pairs, sems)


def ones_beside(values):
    return jnp.concatenate([values, jnp.ones(values.shape, values.dtype)], axis=1)


def read_kernel(owner, lengths, *refs):
    asked, (own_kv, other_kv), pairs, (out_ref, q_ref) = refs[:4], refs[4:6], refs[6:14], refs[14:]
    z, x, c = place()
    step = pl.program_id(0)
    at = z ^ (owner[0] // 4)
    for s in range(4):

        @pl.when(at == s)
        def _(s=s):
            for h in range(4):
                q_ref[h * 64 : (h + 1) * 64, :] = asked[s][:, lanes(step * 512 + h * 128, 128)]

    q = q_ref[...]
    column = lax.broadcasted_iota(jnp.int32, (1, 512), 1)
    found = []

    def add(scores, values):
        peak = row_max(scores)
        total = 0
        for s, v in zip(scores, values):
            total = total + jnp.dot(weights(s, peak), ones_beside(v), preferred_element_type=F32)
        found.append((peak, total))

    for pair, ref in enumerate(pairs):
        scores, values = [], []
        for i in range(2):
            block = ((z ^ (pair % 2 * 2 + i)) * 2 + (x ^ (pair // 2 % 2))) * 2 + (c ^ (pair // 4))
            k, v = ref[i * 1024 : i * 1024 + 512, :], ref[i * 1024 + 512 : (i + 1) * 1024, :]
            scores.append(jnp.where(column < lengths[block], dot_t(q, k), masked_score))
            values.append(v)
        add(scores, values)
    row_at = lax.broadcasted_iota(jnp.int32, (256, 64), 0) % 64 + x * 128 + c * 64
    column = lax.broadcasted_iota(jnp.int32, (256, 64), 1)
    scores, values = [], []
    for ref, core in ((own_kv, c), (other_kv, 1 - c)):
        for i in range(2):
            s = dot_t(q, ref[:, i * 256 : i * 256 + 128])
            scores.append(jnp.where(column + i * 128 + core * 64 <= row_at, s, masked_score))
            values.append(ref[:, i * 256 + 128 : (i + 1) * 256])
    add([jnp.concatenate(scores, axis=1)], [jnp.concatenate(values, axis=0)])
    top = functools.reduce(jnp.maximum, [peak for peak, _ in found])
    scales = [jnp.exp2(peak - top) for peak, _ in found]
    sums = sum(scale * part[:, :128] for scale, (_, part) in zip(scales, found))
    total = sum(scale * part[:, 128:] for scale, (_, part) in zip(scales, found))
    answer = (sums / total).astype(BF16)
    for h in range(4):
        out_ref[:, h * 128 : (h + 1) * 128] = answer[h * 64 : (h + 1) * 64, :]


def project_kernel(*refs):
    near, near_far, side, side_far, w_ref, keep_ref, send_ref, sum_ref = refs
    z, x, c = place()
    t = lax.axis_index("tensor")
    for s in range(4):
        w = w_ref[pl.ds(pl.multiple_of((z ^ s) * 1024, 1024), 1024), :]
        across = [(near, s), (near_far, s), (near, 4) if s == 0 else (side, s - 1), (near_far, 4) if s == 0 else (side_far, s - 1)]
        a = jnp.concatenate([ref[i] for ref, i in across], axis=0)
        product = jnp.dot(a, w, preferred_element_type=F32)
        if s == 0:
            sum_ref[...] = product
        else:
            sum_ref[...] += product
    for r in range(4):
        half, core = x ^ (r // 2), c ^ (r % 2)
        at_row = rows(core * 64, 64)
        quarter = sum_ref[r * 64 : (r + 1) * 64, :]

        @pl.when(half == t)
        def _(quarter=quarter, at_row=at_row):
            keep_ref[at_row, :] = quarter

        @pl.when(half != t)
        def _(quarter=quarter, at_row=at_row):
            send_ref[at_row, :] = quarter.astype(BF16)


def row_max(scores):
    tiles = [s[:, i : i + 128] for s in scores for i in range(0, s.shape[1], 128)]
    peak = jnp.max(functools.reduce(jnp.maximum, tiles), axis=1, keepdims=True)
    return jnp.broadcast_to(peak * LOG_SCALE, (scores[0].shape[0], 128))


def weights(s, peak):
    tiles = [jnp.exp2(s[:, i : i + 128] * LOG_SCALE - peak).astype(BF16) for i in range(0, s.shape[1], 128)]
    return jnp.concatenate(tiles, axis=1)


def own_kernel(q_ref, k_ref, v_ref, *rest):
    o_ref, lse_ref = rest[-2:]
    row = lax.broadcasted_iota(jnp.int32, (256, 256), 0)
    column = lax.broadcasted_iota(jnp.int32, (256, 256), 1)
    lane = lax.broadcasted_iota(jnp.int32, (256, 128), 1)

    def half(r):
        own_v = [ones_beside(v_ref[b * 256 : (b + 1) * 256, :]) for b in range(r + 1)]
        found = jnp.zeros((256, 128), F32)
        for h in range(8):
            q = q_ref[:, h * 128 : (h + 1) * 128]
            scores = []
            for b in range(r + 1):
                s = dot_t(q, k_ref[b * 256 : (b + 1) * 256, :])
                scores.append(jnp.where(column <= row, s, masked_score) if b == r else s)
            peak = row_max(scores)
            total = 0
            for b in range(r + 1):
                total = total + jnp.dot(weights(scores[b], peak), own_v[b], preferred_element_type=F32)
            o_ref[:, h * 128 : (h + 1) * 128] = (total[:, :128] / total[:, 128:]).astype(BF16)
            found = jnp.where(lane == h, peak + jnp.log2(total[:, 128:]), found)
        lse_ref[...] = found

    @pl.when(pl.program_id(1) == 0)
    def _():
        half(0)

    @pl.when(pl.program_id(1) == 1)
    def _():
        half(1)


def anchor_kernel(lengths, q_ref, own_ref, lse_ref, near_ref, far_ref, near_c_ref, far_c_ref, *rest):
    o_ref = rest[-1]
    host = lax.axis_index("hst")
    _, x, c = place()
    near_half = jnp.where(c == 0, near_ref[...], near_c_ref[...])
    far_half = jnp.where(c == 0, far_ref[...], far_c_ref[...])
    anchor_len = jnp.where(host > 0, lengths[0], 0)
    own_len = lengths[host] - pl.program_id(1) * 256
    valid = lax.broadcasted_iota(jnp.int32, (256, 128), 0) < own_len
    column = lax.broadcasted_iota(jnp.int32, (1, 256), 1)
    values = ones_beside(jnp.concatenate([near_half[256:512, :], far_half[256:512, :]], axis=0))
    near_ok, far_ok = column + x * 256 < anchor_len, column + (1 - x) * 256 < anchor_len
    for h in range(8):
        at = slice(h * 128, (h + 1) * 128)
        q = q_ref[:, at]
        near = jnp.where(near_ok, dot_t(q, near_half[0:256, :]), masked_score)
        far = jnp.where(far_ok, dot_t(q, far_half[0:256, :]), masked_score)
        lse = jnp.broadcast_to(lse_ref[:, h : h + 1], (256, 128))
        peak = jnp.maximum(row_max([near, far]), lse)
        w = jnp.concatenate([weights(near, peak), weights(far, peak)], axis=1)
        total = jnp.dot(w, values, preferred_element_type=F32)
        own = jnp.exp2(lse - peak)
        result = (total[:, :128] + own * own_ref[:, at].astype(F32)) / (total[:, 128:] + own)
        o_ref[:, at] = jnp.where(valid, result, 0.0).astype(BF16)


def body(ctx_query, ctx_key, context_value, lengths, owner, ask_query, ask_key, candidate_value_rows, out_weight):
    z, x, c = place()
    ask = [ask_query, ask_key, candidate_value_rows]
    dma = pltpu.SemaphoreType.DMA

    def send(array, pairs):
        return lax.ppermute(array, "hst", pairs)

    def after(array, *others):
        return lax.optimization_barrier((array, *others))[0]

    own_out, lse = None, []

    def own(g, *others):
        nonlocal own_out
        block = pl.BlockSpec((256, 1024), lambda j, i, g=g: (i, 2 * g + j))
        head = pl.BlockSpec((512, 128), lambda j, i, g=g: (0, 2 * g + j))
        own_out, found = call(
            own_kernel, [pltpu.HBM((512, 4096), BF16), pltpu.HBM((1024, 128), F32)],
            [block, head, head] + ([] if g == 0 else [ANY]),
            [block, pl.BlockSpec((256, 128), lambda j, i: (2 * j + i, 0))],
            in_hbm(ctx_query, ctx_key, context_value) + ([] if g == 0 else in_hbm(own_out)),
            after=others, grid=(2, 2), aliases={} if g == 0 else {3: 0}, flops=8 * 4096 * 768 * 256, data=2**22, vmem=16,
        )
        lse.append(found)
        return found

    ctx_out = None

    def encode(g, n, *others):
        nonlocal ctx_out
        block = pl.BlockSpec((256, 1024), lambda j, i, _, g=g: (i, g + j))
        half = pl.BlockSpec((512, 128), lambda j, i, _, g=g: (0, g + j))
        logs = pl.BlockSpec((256, 128), lambda j, i, _, g=g: ((g % 2 + j) * 2 + i, 0))
        ctx_out = call(
            anchor_kernel, pltpu.HBM((512, 4096), BF16),
            [block, block, logs] + [half] * 4 + ([] if g == 0 else [ANY]),
            block,
            in_hbm(ctx_query, own_out, lse[g // 2]) + halves + ([] if g == 0 else in_hbm(ctx_out)),
            scalars=[lengths], after=others, grid=(n, 2), aliases={} if g == 0 else {7: 0},
            flops=n * 4 * 4096 * 512 * 256, data=2**21, vmem=16,
        )
        return ctx_out

    packed = call(
        ask_pack_kernel, shape((128, 5120), BF16), [ANY] * 3, WHOLE, in_hbm(*ask), scratch=[dma((6,))]
    )
    kv = call(
        kv_pack_kernel,
        [pltpu.HBM((1024, 128), BF16)] + [shape((1024, 128), BF16)] * 3 + [pltpu.HBM((512, 512), BF16)] * 2,
        [ANY] * 2, [WHOLE] * 6, in_hbm(ctx_key, context_value), after=[packed], scratch=[dma((12,))],
    )
    got_c = in_hbm(swap(packed, 1))
    kv_z = [kv[0]] + [swap(kv[s], 4 * s) for s in (1, 2, 3)]
    got = send(after(kv[5], packed), [(0, 2)])
    sent = call(
        x_pack_kernel, shape((64, 6144), BF16), [ANY] * 4, WHOLE, got_c + in_hbm(*ask), scalars=[owner],
        scratch=[dma((5,))],
    )
    got_x = swap(sent, 2)

    tick = own(0, sent)
    near = jnp.where(x == 0, kv[4], after(got, tick))
    got = send(near, [(i, i + 8) for i in (0, 2)])
    first = jnp.concatenate([kv[0], after(kv_z[1], tick)], axis=0)
    first_x = swap(first, 2)
    tick = own(1, near, kv_z[1])
    parts = call(
        z_pack_kernel, [shape((64, 1536), BF16)] * 4, [ANY, WHOLE] + [ANY] * 3,
        [WHOLE] * 4, got_c + in_vmem(got_x) + in_hbm(*ask), scalars=[owner], after=[tick], scratch=[dma((20,))],
    )
    asked = [parts[0]] + [swap(parts[s], 4 * s) for s in (1, 2, 3)]
    near = jnp.where(z == 0, near, after(got, parts[0]))
    got = send(near, [(i, i + 4) for i in (0, 2, 8, 10)])
    second = jnp.concatenate([after(kv_z[2], parts[0]), kv_z[3]], axis=0)
    second_x = swap(second, 2)

    level = z ^ (owner[0] // 4)
    own_kv = asked[0][:, 1024:]
    for s in (1, 2, 3):
        own_kv = jnp.where(level == s, asked[s][:, 1024:], own_kv)
    other_kv = swap(own_kv, 1)
    pairs = [first, second, first_x, second_x]
    pairs += [swap(after(part, own_kv), 1) for part in pairs]
    near = jnp.where(z % 2 == 0, near, after(got, own_kv))
    far = swap(near, 2)
    near_c = send(near, [(i, i + 1) for i in range(0, 16, 2)])
    answer = call(
        read_kernel, shape((64, 1024), BF16), [WHOLE] * 14, pl.BlockSpec((64, 512), lambda i, *_: (0, i)),
        in_vmem(*asked, own_kv, other_kv, *pairs),
        scalars=[owner, lengths], grid=(2,),
        scratch=[pltpu.VMEM((256, 128), BF16)], flops=4 * 512 * 8192 * 256, data=2**22, vmem=20,
    )

    far = after(far, answer)
    halves = [near, far, after(near_c, answer), send(far, [(i, i + 1) for i in range(0, 16, 2)])]

    across = [swap(answer, 4 * s) for s in (1, 2, 3)]
    side = swap(answer, 2)
    tick = encode(0, 2, answer)
    across = [after(part, tick) for part in across]
    sides = [swap(part, 2) for part in across]
    near = jnp.stack([answer] + across + [after(side, tick)])
    near_far = swap(near, 1)
    tick = encode(2, 1)
    side = jnp.stack([after(part, tick) for part in sides])
    side_far = swap(side, 1)
    keep, sent = call(
        project_kernel, [shape((128, 512), F32), shape((128, 512), BF16)], [WHOLE] * 5, [WHOLE] * 2,
        in_vmem(near, near_far, side, side_far, out_weight), scratch=[pltpu.VMEM((256, 512), F32)],
        flops=2 * 256 * 4096 * 512, data=2**22, vmem=16,
    )
    got = lax.ppermute(sent, "tensor", [(0, 1), (1, 0)])
    tick = encode(3, 1, sent)
    return ctx_out, (keep + after(got, tick).astype(F32)).astype(BF16)


def solution(mesh):
    placed = (
        P("hst", "tensor"),
        P("hst", "tensor"),
        P("hst", "tensor"),
        P(),
        P(),
        P("hst", None, "tensor"),
        P("hst", None, "tensor"),
        P("hst", None, "tensor"),
        P("tensor", "hst"),
    )
    fits = dict(mesh.shape) == {"hst": 16, "tensor": 2}
    return jax.shard_map(
        body if fits else generic_body,
        mesh=mesh,
        in_specs=placed,
        out_specs=(P("hst", "tensor"), P("tensor", "hst")),
        check_vma=False,
    )
```
